32 devices in a mesh: tm: 4 (over x, core), space: 8 (over z, y).
Axes of the slice: x: 2, y: 2, z: 4, core: 2. Of those that a mesh axis runs over, the one named last changes fastest.
Arguments:
- starts: float32 [4, 4, 64, 8192], P('tm', None, 'space'), may hold values from -6 to 6
- labels: int32 [64, 8192], P('space'), may hold values from 0 to 3
- coef_table: float32 [3, 4], replicated, may hold values from 0.2 to 1.2
Outputs:
- new_starts: float32 [4, 4, 64, 8192], P('tm', None, 'space')
The draws below stay inside these ranges and needn't reach their ends.
All inputs are finite; a program needn't handle non-finite values.
Results may differ from the reference program's by a relative error of at most 0.00015.
Values sent between devices are 32-bit elements; how exact they have to be, the bound alone decides.
A program may use at most 192 MiB of HBM per device.

```python
import math
import jax
import jax.numpy as jnp
from jax import lax

NX = 32
FINE = 4
LABELS = 4
SLICES = 4
NZ = 64
NXY = 8192


def set_ends(values, stream_key, least, top_value):
    longest = values.shape.index(max(values.shape))
    spots = []
    for shift in (0, 1):
        where = [jax.random.randint(jax.random.fold_in(stream_key, axis), (), 0, length) for axis, length in enumerate(values.shape)]
        where[longest] = (where[longest] + shift) % values.shape[longest]
        spots.append(tuple(where))
    return values.at[spots[0]].set(least).at[spots[1]].set(top_value)


def block_levels(rng, dims, cuts, low, largest):
    level, own = 1.0, jax.random.fold_in(rng, 6)
    for position, parts in cuts:
        heights = jnp.exp(jax.random.uniform(jax.random.fold_in(own, position), (parts,), jnp.float32, low / len(cuts), largest / len(cuts)))
        level = level * jnp.repeat(heights, dims[position] // parts).reshape([-1 if axis == position else 1 for axis in range(len(dims))])
    return level


def bell_draw(key, extent, scale, reach, split=(), kind=jnp.bfloat16):
    gain = block_levels(key, extent, split, -0.22, 0.18) if split else 1.0
    drawn = jax.random.normal(key, extent, jnp.float32) * scale * gain
    return jnp.minimum(jnp.maximum(drawn, -reach), reach).astype(kind)


def setup_inputs(seed: int = 0) -> dict:
    splits = jax.random.split(jax.random.key(seed), 4)
    starts = bell_draw(splits[0], (SLICES, 4, NZ, NXY), 1.0, 6.0, ((0, 4), (2, 8)), jnp.float32)
    labels = set_ends(jax.random.randint(splits[1], (NZ, NXY), 0, LABELS), jax.random.fold_in(splits[1], 1), 0, LABELS - 1).astype(jnp.int32)
    coef_table = jnp.clip(jnp.exp(jax.random.uniform(splits[2], (3, LABELS), jnp.float32, math.log(0.2), math.log(1.2))), 0.2, 1.2)
    return dict(starts=starts, labels=labels, coef_table=coef_table)


fine_tau = 0.1
coarse_tau = 0.4

def lookup(labels, table):
    fields = jnp.zeros((3,) + labels.shape, jnp.float32)
    for tissue in range(table.shape[1]):
        chosen = (labels == tissue).astype(jnp.float32)
        fields = fields + table[:, tissue][:, None, None] * chosen[None]
    return fields

def shift_flat(field_in, offset):
    filler = jnp.zeros(field_in.shape[:-1] + (abs(offset),), field_in.dtype)
    if offset > 0:
        return jnp.concatenate([field_in[..., offset:], filler], -1)
    return jnp.concatenate([filler, field_in[..., :offset]], -1)

def biot_update(padded, coefficients, plane_width, tau, spacing):
    field_now = padded[:, 1:-1]
    components, z_depth, plane_cells = field_now.shape
    length = plane_cells // plane_width
    column = lax.broadcasted_iota(jnp.int32, (1, 1, plane_cells), 2) % length
    x_up = shift_flat(field_now, length)
    x_dn = shift_flat(field_now, -length)
    y_up = jnp.where(column != length - 1, shift_flat(field_now, 1), 0.0)
    y_dn = jnp.where(column != 0, shift_flat(field_now, -1), 0.0)
    z_up = padded[:, 2:]
    z_dn = padded[:, :-2]
    laplacian = (x_up + x_dn + y_up + y_dn + z_up + z_dn - 6.0 * field_now) / (spacing * spacing)
    inv_two = 1.0 / (2.0 * spacing)
    grad_x = (x_up[3] - x_dn[3]) * inv_two
    grad_y = (y_up[3] - y_dn[3]) * inv_two
    grad_z = (z_up[3] - z_dn[3]) * inv_two
    divergence = (x_up[0] - x_dn[0] + y_up[1] - y_dn[1] + z_up[2] - z_dn[2]) * inv_two
    shear_field = coefficients[0]
    perm_field = coefficients[1]
    couple_field = coefficients[2]
    shifted_disp = field_now[:3] + tau * (shear_field * laplacian[:3] - couple_field * jnp.stack([grad_x, grad_y, grad_z]))
    pressure = field_now[3] + tau * (perm_field * laplacian[3] - couple_field * divergence)
    return jnp.concatenate([shifted_disp, pressure[None]], 0)

def restrict(field_in, plane_width):
    components, z_depth, plane_cells = field_in.shape
    length = plane_cells // plane_width
    blocks = field_in.reshape(components, z_depth // 2, 2, plane_width // 2, 2, length // 2, 2)
    return blocks.sum(axis=(2, 4, 6)).reshape(components, z_depth // 2, -1) * 0.125

def prolong(field_in, plane_width):
    components, z_depth, plane_cells = field_in.shape
    length = plane_cells // plane_width
    shaped = field_in.reshape(components, z_depth, 1, plane_width, 1, length, 1)
    spread = jnp.broadcast_to(shaped, (components, z_depth, 2, plane_width, 2, length, 2))
    return spread.reshape(components, 2 * z_depth, 4 * plane_cells)

def substitute(factor, right_side):
    order = factor.shape[0]
    forward = []
    for row_index in range(order):
        running = right_side[row_index]
        for column in range(row_index):
            running = running - factor[row_index, column] * forward[column]
        forward.append(running / factor[row_index, row_index])
    backward = [None] * order
    for row_index in reversed(range(order)):
        running = forward[row_index]
        for column in range(row_index + 1, order):
            running = running - factor[column, row_index] * backward[column]
        backward[row_index] = running / factor[row_index, row_index]
    return jnp.stack(backward)

def pad_z(field_in):
    return jnp.pad(field_in, ((0, 0), (1, 1), (0, 0)))

def reference(starts, labels, coef_table):
    highest = lax.Precision.HIGHEST
    coefficients = lookup(labels, coef_table)
    coarse_coefs = restrict(coefficients, NX)
    end_fields = []
    coarse_starts = []
    coarse_ends = []
    for slice_index in range(SLICES):
        field_now = starts[slice_index]
        for fine_step in range(FINE):
            field_now = biot_update(pad_z(field_now), coefficients, NX, fine_tau, 1.0)
        end_fields.append(field_now)
        coarse_starts.append(restrict(starts[slice_index], NX))
        coarse_ends.append(restrict(field_now, NX))
    all_ru = jnp.stack(coarse_starts)
    all_rf = jnp.stack(coarse_ends)
    flat_ru = all_ru.reshape(SLICES, -1)
    flat_rf = all_rf.reshape(SLICES, -1)
    gram = jnp.dot(flat_ru, flat_ru.T, precision=highest)
    factor = jnp.linalg.cholesky(gram)
    defect = jnp.zeros_like(coarse_starts[0])
    updated = []
    for slice_index in range(SLICES):
        inner_products = jnp.dot(flat_ru, defect.reshape(-1), precision=highest)
        weights = substitute(factor, inner_products)
        remainder = defect - jnp.dot(weights, flat_ru, precision=highest).reshape(defect.shape)
        image = biot_update(pad_z(remainder), coarse_coefs, NX // 2, coarse_tau, 2.0)
        correction = image + jnp.dot(weights, flat_rf, precision=highest).reshape(defect.shape)
        updated.append(end_fields[slice_index] + prolong(correction, NX // 2))
        if slice_index + 1 < SLICES:
            defect = all_rf[slice_index] + correction - all_ru[slice_index + 1]
    return jnp.stack(updated)
```

```python
import functools
import jax
import jax.numpy as jnp
from jax import lax
from jax.experimental import pallas as pl
from jax.experimental.pallas import tpu as pltpu
from jax.sharding import PartitionSpec as P

NX = 32
FINE = 4
CHUNKS = 4
BLOCK = 4

fine_tau = 0.1
coarse_tau = 0.4
MESH = pl.DeviceIdType.MESH


def kernel(
    slices, spaces, starts_ref, labels_ref, table_ref, out_ref,
    field_a, field_b, coefs, halo, pair_lo, pair_hi, coarse_coefs,
    all_ru, all_rf, gram_buf, dot_buf, padded, expanded, layer_out, layer_in, defect_ref, corr_ref,
    halo_send, halo_recv, ru_send, ru_recv, rf_send, rf_recv,
    gram_send, gram_recv, dot_send, dot_recv, layer_send, layer_recv,
):
    tm = lax.axis_index("tm")
    me = lax.axis_index("space")
    length = starts_ref.shape[-1] // NX
    depth = starts_ref.shape[2]
    half = NX // 2
    rows = half * depth // 2
    f32 = jnp.float32

    barrier = pltpu.get_barrier_semaphore()
    for off in range(1, slices):
        pl.semaphore_signal(
            barrier, inc=1, device_id={"tm": lax.rem(tm + off, slices)}, device_id_type=MESH
        )
    for off in range(1, spaces):
        pl.semaphore_signal(
            barrier, inc=1, device_id={"space": lax.rem(me + off, spaces)}, device_id_type=MESH
        )

    has_down = me > 0
    has_up = me < spaces - 1

    zero_plane = jnp.zeros((4, 1, depth, length), f32)
    for buf in (field_a, field_b):
        buf[:, pl.ds(0, 1)] = zero_plane
        buf[:, pl.ds(NX + 1, 1)] = zero_plane

    def load(x, carry):
        cols = pl.ds(pl.multiple_of(x * length, length), length)
        field_a[:, x + 1] = starts_ref[0, :, :, cols]
        return carry

    lax.fori_loop(0, NX, load, 0, unroll=4)

    pl.semaphore_wait(barrier, slices - 1 + spaces - 1)

    span = NX // CHUNKS

    def halo_copies(step, chunk, buf):
        xs = pl.ds(1 + chunk * span, span)
        to = pl.ds(chunk * span, span)
        up = pltpu.make_async_remote_copy(
            src_ref=buf.at[:, xs, pl.ds(depth - 1, 1), :],
            dst_ref=halo.at[step, 0, :, to],
            send_sem=halo_send.at[step, 0, chunk],
            recv_sem=halo_recv.at[step, 0, chunk],
            device_id={"space": lax.rem(me + 1, spaces)},
            device_id_type=MESH,
        )
        down = pltpu.make_async_remote_copy(
            src_ref=buf.at[:, xs, pl.ds(0, 1), :],
            dst_ref=halo.at[step, 1, :, to],
            send_sem=halo_send.at[step, 1, chunk],
            recv_sem=halo_recv.at[step, 1, chunk],
            device_id={"space": lax.rem(me + spaces - 1, spaces)},
            device_id_type=MESH,
        )
        return up, down

    def start_pair(pair):
        @pl.when(has_up)
        def _():
            pair[0].start()

        @pl.when(has_down)
        def _():
            pair[1].start()

    def wait_pair(pair):
        @pl.when(has_up)
        def _():
            pair[0].wait_send()
            pair[1].wait_recv()

        @pl.when(has_down)
        def _():
            pair[1].wait_send()
            pair[0].wait_recv()

    for chunk in range(CHUNKS):
        start_pair(halo_copies(0, chunk, field_a))

    @pl.when(jnp.logical_not(has_down))
    def _():
        for step in range(FINE):
            halo[step, 0] = jnp.zeros(halo.shape[2:], f32)
        for turn in range(slices - 1):
            layer_in[turn, 0] = jnp.zeros(layer_in.shape[2:], f32)

    @pl.when(jnp.logical_not(has_up))
    def _():
        for step in range(FINE):
            halo[step, 1] = jnp.zeros(halo.shape[2:], f32)
        for turn in range(slices - 1):
            layer_in[turn, 1] = jnp.zeros(layer_in.shape[2:], f32)

    scales = (fine_tau, fine_tau, fine_tau * 0.5)

    def fill(x, carry):
        cols = pl.ds(pl.multiple_of(x * length, length), length)
        labels = labels_ref[:, cols]
        for k in range(3):
            value = jnp.zeros(labels.shape, f32)
            for tissue in range(table_ref.shape[1]):
                value = jnp.where(labels == tissue, table_ref[k, tissue] * scales[k], value)
            coefs[k, x] = value
        return carry

    lax.fori_loop(0, NX, fill, 0, unroll=2)

    lane = lax.broadcasted_iota(jnp.int32, (length // 2, length // 2), 0)
    place = lax.broadcasted_iota(jnp.int32, (length // 2, length // 2), 1)
    quarter = length // 4
    pick_lo = jnp.where(lane // 2 == place, 0.125, 0.0).astype(f32)
    pick_hi = jnp.where(lane // 2 + quarter == place, 0.125, 0.0).astype(f32)

    def restrict(buf, first, count):
        def pair_up(i, carry):
            for c in range(count):
                both = buf[c, first + 2 * i] + buf[c, first + 2 * i + 1]
                at = pl.ds(pl.multiple_of((c * half + i) * depth, depth), depth)
                pair_lo[at, :] = both[:, : length // 2]
                pair_hi[at, :] = both[:, length // 2 :]
            return carry

        lax.fori_loop(0, half, pair_up, 0, unroll=4)
        even = pl.ds(0, count * rows, stride=2)
        odd = pl.ds(1, count * rows, stride=2)
        low = pair_lo[even, :] + pair_lo[odd, :]
        high = pair_hi[even, :] + pair_hi[odd, :]
        dot = functools.partial(
            jnp.dot, precision=lax.Precision.HIGHEST, preferred_element_type=f32
        )
        return dot(low, pick_lo) + dot(high, pick_hi)

    def gather_copies(buf, sends, recvs):
        return [
            pltpu.make_async_remote_copy(
                src_ref=buf.at[tm], dst_ref=buf.at[tm],
                send_sem=sends.at[off - 1], recv_sem=recvs.at[off - 1],
                device_id={"tm": lax.rem(tm + off, slices)}, device_id_type=MESH,
            )
            for off in range(1, slices)
        ]

    def space_copies(part, sends, recvs):
        return [
            pltpu.make_async_remote_copy(
                src_ref=part, dst_ref=part,
                send_sem=sends.at[off - 1], recv_sem=recvs.at[off - 1],
                device_id={"space": lax.rem(me + off, spaces)}, device_id_type=MESH,
            )
            for off in range(1, spaces)
        ]

    all_ru[tm] = restrict(field_a, 1, 4)
    ru_copies = gather_copies(all_ru, ru_send, ru_recv)
    for copy in ru_copies:
        copy.start()

    coarse_coefs[...] = restrict(coefs, 0, 3)

    row = lax.broadcasted_iota(jnp.int32, (1, depth, length), 1)
    col = lax.broadcasted_iota(jnp.int32, (1, depth, length), 2)
    gram_copies = None
    bufs = (field_a, field_b)
    for step in range(FINE):
        src, dst = bufs[step % 2], bufs[(step + 1) % 2]
        for chunk in range(CHUNKS):
            wait_pair(halo_copies(step, chunk, src))

            def block(b, carry):
                x0 = chunk * span + b * BLOCK
                now, dx, dy, dz, lap = [], [], [], [], []
                for c in range(4):
                    v = src[c, pl.ds(x0 + 1, BLOCK)]
                    x_up = src[c, pl.ds(x0 + 2, BLOCK)]
                    x_dn = src[c, pl.ds(x0, BLOCK)]
                    y_up = jnp.where(col == length - 1, 0.0, pltpu.roll(v, length - 1, 2))
                    y_dn = jnp.where(col == 0, 0.0, pltpu.roll(v, 1, 2))
                    z_up = jnp.where(
                        row == depth - 1, halo[step, 1, c, pl.ds(x0, BLOCK)], pltpu.roll(v, depth - 1, 1)
                    )
                    z_dn = jnp.where(row == 0, halo[step, 0, c, pl.ds(x0, BLOCK)], pltpu.roll(v, 1, 1))
                    now.append(v)
                    lap.append(x_up + x_dn + y_up + y_dn + z_up + z_dn - 6.0 * v)
                    if c in (0, 3):
                        dx.append(x_up - x_dn)
                    if c in (1, 3):
                        dy.append(y_up - y_dn)
                    if c in (2, 3):
                        dz.append(z_up - z_dn)
                shear = coefs[0, pl.ds(x0, BLOCK)]
                perm = coefs[1, pl.ds(x0, BLOCK)]
                couple = coefs[2, pl.ds(x0, BLOCK)]
                grads = (dx[1], dy[1], dz[1])
                for c in range(3):
                    dst[c, pl.ds(x0 + 1, BLOCK)] = now[c] + (shear * lap[c] - couple * grads[c])
                dst[3, pl.ds(x0 + 1, BLOCK)] = now[3] + (
                    perm * lap[3] - couple * (dx[0] + dy[0] + dz[0])
                )
                return carry

            lax.fori_loop(0, span // BLOCK, block, 0)
            if step + 1 < FINE:
                start_pair(halo_copies(step + 1, chunk, dst))
        if step == FINE - 2:
            for copy in ru_copies:
                copy.wait()
            line = 0
            for a in range(slices):
                for b in range(a + 1):
                    gram_buf[me, pl.ds(line, 1), :] = jnp.sum(
                        all_ru[a] * all_ru[b], axis=0, keepdims=True
                    )
                    line += 1
            for spare in range(line, gram_buf.shape[1]):
                gram_buf[me, pl.ds(spare, 1), :] = jnp.zeros((1, length // 2), f32)
            gram_copies = space_copies(gram_buf.at[me], gram_send, gram_recv)
            for copy in gram_copies:
                copy.start()
    final = bufs[FINE % 2]

    all_rf[tm] = restrict(final, 1, 4)
    rf_copies = gather_copies(all_rf, rf_send, rf_recv)
    for copy in rf_copies:
        copy.start()

    def total(buf):
        summed = buf[0]
        for s in range(1, spaces):
            summed = summed + buf[s]
        return jnp.broadcast_to(jnp.sum(summed, axis=1, keepdims=True), summed.shape)

    for copy in gram_copies:
        copy.wait()
    gram = total(gram_buf)
    entry = {}
    line = 0
    for a in range(slices):
        for b in range(a + 1):
            entry[a, b] = gram[line : line + 1]
            line += 1
    factor, inverse = {}, {}
    for b in range(slices):
        diag = entry[b, b]
        for k in range(b):
            diag = diag - factor[b, k] * factor[b, k]
        factor[b, b] = jnp.sqrt(diag)
        inverse[b] = 1.0 / factor[b, b]
        for a in range(b + 1, slices):
            value = entry[a, b]
            for k in range(b):
                value = value - factor[a, k] * factor[b, k]
            factor[a, b] = value * inverse[b]

    padded[...] = jnp.zeros(padded.shape, f32)
    corr_ref[...] = jnp.zeros(corr_ref.shape, f32)
    for copy in rf_copies:
        copy.wait()

    crow = lax.broadcasted_iota(jnp.int32, (rows, length // 2), 0)
    ccol = lax.broadcasted_iota(jnp.int32, (rows, length // 2), 1)
    per = depth // 2
    at_top = lax.rem(crow, per) == per - 1
    at_bottom = lax.rem(crow, per) == 0
    layers = 4 * half

    def coarse_part(k):
        return coarse_coefs[pl.ds(k * rows, rows), :]

    lap_scale = coarse_tau / 4.0 / fine_tau
    div_scale = coarse_tau / 4.0 / (fine_tau * 0.5)

    defect_ref[...] = all_rf[0] - all_ru[1]
    for j in range(1, slices):
        turn = j - 1
        defect = defect_ref[...]
        for a in range(slices):
            dot_buf[turn, me, pl.ds(a, 1), :] = jnp.sum(all_ru[a] * defect, axis=0, keepdims=True)
        for spare in range(slices, dot_buf.shape[2]):
            dot_buf[turn, me, pl.ds(spare, 1), :] = jnp.zeros((1, length // 2), f32)
        copies = space_copies(dot_buf.at[turn, me], dot_send.at[turn], dot_recv.at[turn])
        for copy in copies:
            copy.start()
        for copy in copies:
            copy.wait()
        inner = total(dot_buf.at[turn])
        forward, weights = [], [None] * slices
        for a in range(slices):
            value = inner[a : a + 1]
            for k in range(a):
                value = value - factor[a, k] * forward[k]
            forward.append(value * inverse[a])
        for a in reversed(range(slices)):
            value = forward[a]
            for k in range(a + 1, slices):
                value = value - factor[k, a] * weights[k]
            weights[a] = value * inverse[a]

        rest = defect
        for a in range(slices):
            rest = rest - weights[a] * all_ru[a]
        defect_ref[...] = rest
        layer_out[turn, 0] = defect_ref[pl.ds(per - 1, layers, stride=per), :]
        layer_out[turn, 1] = defect_ref[pl.ds(0, layers, stride=per), :]
        pair = [
            pltpu.make_async_remote_copy(
                src_ref=layer_out.at[turn, way], dst_ref=layer_in.at[turn, way],
                send_sem=layer_send.at[turn, way], recv_sem=layer_recv.at[turn, way],
                device_id={"space": lax.rem(me + by, spaces)}, device_id_type=MESH,
            )
            for way, by in ((0, 1), (1, spaces - 1))
        ]
        start_pair(pair)
        for c in range(4):
            padded[c, pl.ds(8, rows), :] = rest[c * rows : (c + 1) * rows]
        blend = weights[0] * all_rf[0]
        for a in range(1, slices):
            blend = blend + weights[a] * all_rf[a]
        wait_pair(pair)
        expanded[0, pl.ds(0, layers, stride=per), :] = layer_in[turn, 0]
        expanded[1, pl.ds(per - 1, layers, stride=per), :] = layer_in[turn, 1]
        now, dx, dy, dz, lap = [], [], [], [], []
        width = length // 2
        for c in range(4):
            v = padded[c, pl.ds(8, rows), :]
            x_up = padded[c, pl.ds(8 + per, rows), :]
            x_dn = padded[c, pl.ds(8 - per, rows), :]
            y_up = jnp.where(ccol == width - 1, 0.0, pltpu.roll(v, width - 1, 1))
            y_dn = jnp.where(ccol == 0, 0.0, pltpu.roll(v, 1, 1))
            z_up = jnp.where(at_top, expanded[1, pl.ds(c * rows, rows), :], padded[c, pl.ds(9, rows), :])
            z_dn = jnp.where(at_bottom, expanded[0, pl.ds(c * rows, rows), :], padded[c, pl.ds(7, rows), :])
            now.append(v)
            lap.append((x_up + x_dn + y_up + y_dn + z_up + z_dn - 6.0 * v) * lap_scale)
            if c in (0, 3):
                dx.append(x_up - x_dn)
            if c in (1, 3):
                dy.append(y_up - y_dn)
            if c in (2, 3):
                dz.append(z_up - z_dn)
        couple = coarse_part(2) * div_scale
        grads = (dx[1], dy[1], dz[1])
        parts = [now[c] + (coarse_part(0) * lap[c] - couple * grads[c]) for c in range(3)]
        parts.append(now[3] + (coarse_part(1) * lap[3] - couple * (dx[0] + dy[0] + dz[0])))
        corr = jnp.concatenate(parts, axis=0) + blend

        @pl.when(tm == j)
        def _():
            corr_ref[...] = corr

        if j + 1 < slices:
            defect_ref[...] = all_rf[j] + corr - all_ru[j + 1]

    spread_lo = jnp.where(lane == place // 2, 1.0, 0.0).astype(f32)
    spread_hi = jnp.where(lane == place // 2 + quarter, 1.0, 0.0).astype(f32)
    own = corr_ref[...]
    for buf, spread in ((pair_lo, spread_lo), (pair_hi, spread_hi)):
        wide = jnp.dot(own, spread, precision=lax.Precision.HIGHEST, preferred_element_type=f32)
        buf[pl.ds(0, 4 * rows, stride=2), :] = wide
        buf[pl.ds(1, 4 * rows, stride=2), :] = wide

    def finish(i, carry):
        for c in range(4):
            at = pl.ds(pl.multiple_of((c * half + i) * depth, depth), depth)
            add = jnp.concatenate([pair_lo[at, :], pair_hi[at, :]], axis=1)
            for k in range(2):
                cols = pl.ds(pl.multiple_of((2 * i + k) * length, length), length)
                out_ref[0, c, :, cols] = final[c, 2 * i + k + 1] + add
        return carry

    lax.fori_loop(0, half, finish, 0, unroll=2)


def shards(slices, spaces, starts, labels, coef_table):
    f32 = jnp.float32
    depth, plane = starts.shape[2:]
    length = plane // NX
    width = length // 2
    half = NX // 2
    rows = half * depth // 2
    gram_rows = -(-(slices * (slices + 1) // 2) // 8) * 8
    dot_rows = -(-slices // 8) * 8
    vmem = pl.BlockSpec(memory_space=pltpu.VMEM)
    dma = pltpu.SemaphoreType.DMA
    return pl.pallas_call(
        functools.partial(kernel, slices, spaces),
        out_shape=jax.ShapeDtypeStruct(starts.shape, f32),
        in_specs=[vmem, vmem, pl.BlockSpec(memory_space=pltpu.SMEM)],
        out_specs=vmem,
        scratch_shapes=[
            pltpu.VMEM((4, NX + 2, depth, length), f32),
            pltpu.VMEM((4, NX + 2, depth, length), f32),
            pltpu.VMEM((3, NX, depth, length), f32),
            pltpu.VMEM((FINE, 2, 4, NX, 1, length), f32),
            pltpu.VMEM((8 * rows, width), f32),
            pltpu.VMEM((8 * rows, width), f32),
            pltpu.VMEM((3 * rows, width), f32),
            pltpu.VMEM((slices, 4 * rows, width), f32),
            pltpu.VMEM((slices, 4 * rows, width), f32),
            pltpu.VMEM((spaces, gram_rows, width), f32),
            pltpu.VMEM((slices - 1, spaces, dot_rows, width), f32),
            pltpu.VMEM((4, rows + 16, width), f32),
            pltpu.VMEM((2, 4 * rows, width), f32),
            pltpu.VMEM((slices - 1, 2, 4 * half, width), f32),
            pltpu.VMEM((slices - 1, 2, 4 * half, width), f32),
            pltpu.VMEM((4 * rows, width), f32),
            pltpu.VMEM((4 * rows, width), f32),
            dma((FINE, 2, CHUNKS)),
            dma((FINE, 2, CHUNKS)),
            dma((slices - 1,)),
            dma((slices - 1,)),
            dma((slices - 1,)),
            dma((slices - 1,)),
            dma((spaces - 1,)),
            dma((spaces - 1,)),
            dma((slices - 1, spaces - 1)),
            dma((slices - 1, spaces - 1)),
            dma((slices - 1, 2)),
            dma((slices - 1, 2)),
        ],
        compiler_params=pltpu.CompilerParams(
            collective_id=0, has_side_effects=True, vmem_limit_bytes=48 * 1024 * 1024
        ),
    )(starts, labels, coef_table)


def solution(mesh):
    placed = (P("tm", None, "space", None), P("space", None), P())
    return jax.shard_map(
        functools.partial(shards, mesh.shape["tm"], mesh.shape["space"]),
        mesh=mesh, in_specs=placed, out_specs=P("tm", None, "space", None), check_vma=False,
    )
```

```python
import functools
import jax
import jax.numpy as jnp
from jax import lax
from jax.experimental import pallas as pl
from jax.experimental.pallas import tpu as pltpu
from jax.sharding import PartitionSpec as P

NX = 32
FINE = 4
CHUNKS = 4
BLOCK = 4

fine_tau = 0.1
coarse_tau = 0.4
MESH = pl.DeviceIdType.MESH


def kernel(
    slices, spaces, starts_hbm, labels_hbm, table_ref, out_ref,
    starts_ref, labels_ref,
    field_a, field_b, coefs, halo, pair_lo, pair_hi, coarse_coefs,
    all_ru, all_rf, gram_buf, dot_buf, padded, expanded, layer_out, layer_in, defect_ref, corr_ref,
    halo_send, halo_recv, ru_send, ru_recv, rf_send, rf_recv,
    gram_send, gram_recv, dot_send, dot_recv, layer_send, layer_recv,
    edges_out, all_edges, images, fetch_sem, edge_send, edge_recv, edges_send, edges_recv,
):
    tm = lax.axis_index("tm")
    me = lax.axis_index("space")
    length = starts_ref.shape[-1] // NX
    depth = starts_ref.shape[2]
    half = NX // 2
    rows = half * depth // 2
    f32 = jnp.float32

    fetch = (
        pltpu.make_async_copy(starts_hbm, starts_ref, fetch_sem.at[0]),
        pltpu.make_async_copy(labels_hbm, labels_ref, fetch_sem.at[1]),
    )
    for copy in fetch:
        copy.start()
    barrier = pltpu.get_barrier_semaphore()
    for off in range(1, slices):
        pl.semaphore_signal(
            barrier, inc=1, device_id={"tm": lax.rem(tm + off, slices)}, device_id_type=MESH
        )
    for off in range(1, spaces):
        pl.semaphore_signal(
            barrier, inc=1, device_id={"space": lax.rem(me + off, spaces)}, device_id_type=MESH
        )

    has_down = me > 0
    has_up = me < spaces - 1

    zero_plane = jnp.zeros((4, 1, depth, length), f32)
    for buf in (field_a, field_b):
        buf[:, pl.ds(0, 1)] = zero_plane
        buf[:, pl.ds(NX + 1, 1)] = zero_plane

    fetch[0].wait()

    def load(x, carry):
        cols = pl.ds(pl.multiple_of(x * length, length), length)
        field_a[:, x + 1] = starts_ref[0, :, :, cols]
        return carry

    lax.fori_loop(0, NX, load, 0, unroll=4)

    span = NX // CHUNKS

    def halo_copies(step, chunk, buf):
        xs = pl.ds(1 + chunk * span, span)
        to = pl.ds(chunk * span, span)
        up = pltpu.make_async_remote_copy(
            src_ref=buf.at[:, xs, pl.ds(depth - 1, 1), :],
            dst_ref=halo.at[step, 0, :, to],
            send_sem=halo_send.at[step, 0, chunk],
            recv_sem=halo_recv.at[step, 0, chunk],
            device_id={"space": lax.rem(me + 1, spaces)},
            device_id_type=MESH,
        )
        down = pltpu.make_async_remote_copy(
            src_ref=buf.at[:, xs, pl.ds(0, 1), :],
            dst_ref=halo.at[step, 1, :, to],
            send_sem=halo_send.at[step, 1, chunk],
            recv_sem=halo_recv.at[step, 1, chunk],
            device_id={"space": lax.rem(me + spaces - 1, spaces)},
            device_id_type=MESH,
        )
        return up, down

    def start_pair(pair):
        @pl.when(has_up)
        def _():
            pair[0].start()

        @pl.when(has_down)
        def _():
            pair[1].start()

    def wait_pair(pair):
        @pl.when(has_up)
        def _():
            pair[0].wait_send()
            pair[1].wait_recv()

        @pl.when(has_down)
        def _():
            pair[1].wait_send()
            pair[0].wait_recv()

    @pl.when(jnp.logical_not(has_down))
    def _():
        for step in range(FINE):
            halo[step, 0] = jnp.zeros(halo.shape[2:], f32)
        for turn in range(slices - 1):
            layer_in[turn, 0] = jnp.zeros(layer_in.shape[2:], f32)
        all_edges[tm, 0] = jnp.zeros(all_edges.shape[2:], f32)

    @pl.when(jnp.logical_not(has_up))
    def _():
        for step in range(FINE):
            halo[step, 1] = jnp.zeros(halo.shape[2:], f32)
        for turn in range(slices - 1):
            layer_in[turn, 1] = jnp.zeros(layer_in.shape[2:], f32)
        all_edges[tm, 1] = jnp.zeros(all_edges.shape[2:], f32)

    fetch[1].wait()
    scales = (fine_tau, fine_tau, fine_tau * 0.5)

    def fill(x, carry):
        cols = pl.ds(pl.multiple_of(x * length, length), length)
        labels = labels_ref[:, cols]
        for k in range(3):
            value = jnp.zeros(labels.shape, f32)
            for tissue in range(table_ref.shape[1]):
                value = jnp.where(labels == tissue, table_ref[k, tissue] * scales[k], value)
            coefs[k, x] = value
        return carry

    lax.fori_loop(0, NX, fill, 0, unroll=2)

    lane = lax.broadcasted_iota(jnp.int32, (length // 2, length // 2), 0)
    place = lax.broadcasted_iota(jnp.int32, (length // 2, length // 2), 1)
    quarter = length // 4
    pick_lo = jnp.where(lane // 2 == place, 0.125, 0.0).astype(f32)
    pick_hi = jnp.where(lane // 2 + quarter == place, 0.125, 0.0).astype(f32)

    def restrict(buf, first, count):
        def pair_up(i, carry):
            for c in range(count):
                both = buf[c, first + 2 * i] + buf[c, first + 2 * i + 1]
                at = pl.ds(pl.multiple_of((c * half + i) * depth, depth), depth)
                pair_lo[at, :] = both[:, : length // 2]
                pair_hi[at, :] = both[:, length // 2 :]
            return carry

        lax.fori_loop(0, half, pair_up, 0, unroll=4)
        even = pl.ds(0, count * rows, stride=2)
        odd = pl.ds(1, count * rows, stride=2)
        low = pair_lo[even, :] + pair_lo[odd, :]
        high = pair_hi[even, :] + pair_hi[odd, :]
        dot = functools.partial(
            jnp.dot, precision=lax.Precision.HIGHEST, preferred_element_type=f32
        )
        return dot(low, pick_lo) + dot(high, pick_hi)

    def gather_copies(buf, sends, recvs):
        return [
            pltpu.make_async_remote_copy(
                src_ref=buf.at[tm], dst_ref=buf.at[tm],
                send_sem=sends.at[off - 1], recv_sem=recvs.at[off - 1],
                device_id={"tm": lax.rem(tm + off, slices)}, device_id_type=MESH,
            )
            for off in range(1, slices)
        ]

    def space_copies(part, sends, recvs):
        return [
            pltpu.make_async_remote_copy(
                src_ref=part, dst_ref=part,
                send_sem=sends.at[off - 1], recv_sem=recvs.at[off - 1],
                device_id={"space": lax.rem(me + off, spaces)}, device_id_type=MESH,
            )
            for off in range(1, spaces)
        ]

    per = depth // 2
    layers = 4 * half
    own_start = restrict(field_a, 1, 4)
    all_ru[tm] = own_start
    defect_ref[...] = own_start
    edges_out[0] = defect_ref[pl.ds(per - 1, layers, stride=per), :]
    edges_out[1] = defect_ref[pl.ds(0, layers, stride=per), :]
    coarse_coefs[...] = restrict(coefs, 0, 3)
    padded[...] = jnp.zeros(padded.shape, f32)
    corr_ref[...] = jnp.zeros(corr_ref.shape, f32)

    pl.semaphore_wait(barrier, slices - 1 + spaces - 1)
    for chunk in range(CHUNKS):
        start_pair(halo_copies(0, chunk, field_a))
    edge_pair = [
        pltpu.make_async_remote_copy(
            src_ref=edges_out.at[way], dst_ref=all_edges.at[tm, way],
            send_sem=edge_send.at[way], recv_sem=edge_recv.at[way],
            device_id={"space": lax.rem(me + by, spaces)}, device_id_type=MESH,
        )
        for way, by in ((0, 1), (1, spaces - 1))
    ]
    start_pair(edge_pair)
    ru_copies = gather_copies(all_ru, ru_send, ru_recv)
    for copy in ru_copies:
        copy.start()

    crow = lax.broadcasted_iota(jnp.int32, (rows, length // 2), 0)
    ccol = lax.broadcasted_iota(jnp.int32, (rows, length // 2), 1)
    at_top = lax.rem(crow, per) == per - 1
    at_bottom = lax.rem(crow, per) == 0
    lap_scale = coarse_tau / 4.0 / fine_tau
    div_scale = coarse_tau / 4.0 / (fine_tau * 0.5)

    def coarse_part(k):
        return coarse_coefs[pl.ds(k * rows, rows), :]

    def coarse_image(edges):
        expanded[0, pl.ds(0, layers, stride=per), :] = edges[0]
        expanded[1, pl.ds(per - 1, layers, stride=per), :] = edges[1]
        now, dx, dy, dz, lap = [], [], [], [], []
        width = length // 2
        for c in range(4):
            v = padded[c, pl.ds(8, rows), :]
            x_up = padded[c, pl.ds(8 + per, rows), :]
            x_dn = padded[c, pl.ds(8 - per, rows), :]
            y_up = jnp.where(ccol == width - 1, 0.0, pltpu.roll(v, width - 1, 1))
            y_dn = jnp.where(ccol == 0, 0.0, pltpu.roll(v, 1, 1))
            z_up = jnp.where(at_top, expanded[1, pl.ds(c * rows, rows), :], padded[c, pl.ds(9, rows), :])
            z_dn = jnp.where(at_bottom, expanded[0, pl.ds(c * rows, rows), :], padded[c, pl.ds(7, rows), :])
            now.append(v)
            lap.append((x_up + x_dn + y_up + y_dn + z_up + z_dn - 6.0 * v) * lap_scale)
            if c in (0, 3):
                dx.append(x_up - x_dn)
            if c in (1, 3):
                dy.append(y_up - y_dn)
            if c in (2, 3):
                dz.append(z_up - z_dn)
        couple = coarse_part(2) * div_scale
        grads = (dx[1], dy[1], dz[1])
        parts = [now[c] + (coarse_part(0) * lap[c] - couple * grads[c]) for c in range(3)]
        parts.append(now[3] + (coarse_part(1) * lap[3] - couple * (dx[0] + dy[0] + dz[0])))
        return jnp.concatenate(parts, axis=0)

    edges_copies = gather_copies(all_edges, edges_send, edges_recv)

    row = lax.broadcasted_iota(jnp.int32, (1, depth, length), 1)
    col = lax.broadcasted_iota(jnp.int32, (1, depth, length), 2)
    gram_copies = None
    bufs = (field_a, field_b)
    for step in range(FINE):
        src, dst = bufs[step % 2], bufs[(step + 1) % 2]
        for chunk in range(CHUNKS):
            wait_pair(halo_copies(step, chunk, src))

            def block(b, carry):
                x0 = chunk * span + b * BLOCK
                now, dx, dy, dz, lap = [], [], [], [], []
                for c in range(4):
                    v = src[c, pl.ds(x0 + 1, BLOCK)]
                    x_up = src[c, pl.ds(x0 + 2, BLOCK)]
                    x_dn = src[c, pl.ds(x0, BLOCK)]
                    y_up = jnp.where(col == length - 1, 0.0, pltpu.roll(v, length - 1, 2))
                    y_dn = jnp.where(col == 0, 0.0, pltpu.roll(v, 1, 2))
                    z_up = jnp.where(
                        row == depth - 1, halo[step, 1, c, pl.ds(x0, BLOCK)], pltpu.roll(v, depth - 1, 1)
                    )
                    z_dn = jnp.where(row == 0, halo[step, 0, c, pl.ds(x0, BLOCK)], pltpu.roll(v, 1, 1))
                    now.append(v)
                    lap.append(x_up + x_dn + y_up + y_dn + z_up + z_dn - 6.0 * v)
                    if c in (0, 3):
                        dx.append(x_up - x_dn)
                    if c in (1, 3):
                        dy.append(y_up - y_dn)
                    if c in (2, 3):
                        dz.append(z_up - z_dn)
                shear = coefs[0, pl.ds(x0, BLOCK)]
                perm = coefs[1, pl.ds(x0, BLOCK)]
                couple = coefs[2, pl.ds(x0, BLOCK)]
                grads = (dx[1], dy[1], dz[1])
                for c in range(3):
                    dst[c, pl.ds(x0 + 1, BLOCK)] = now[c] + (shear * lap[c] - couple * grads[c])
                dst[3, pl.ds(x0 + 1, BLOCK)] = now[3] + (
                    perm * lap[3] - couple * (dx[0] + dy[0] + dz[0])
                )
                return carry

            lax.fori_loop(0, span // BLOCK, block, 0)
            if step + 1 < FINE:
                start_pair(halo_copies(step + 1, chunk, dst))
        if step == 0:
            wait_pair(edge_pair)
            for copy in edges_copies:
                copy.start()
        if step == FINE - 2:
            for copy in ru_copies:
                copy.wait()
            line = 0
            for a in range(slices):
                for b in range(a + 1):
                    gram_buf[me, pl.ds(line, 1), :] = jnp.sum(
                        all_ru[a] * all_ru[b], axis=0, keepdims=True
                    )
                    line += 1
            for spare in range(line, gram_buf.shape[1]):
                gram_buf[me, pl.ds(spare, 1), :] = jnp.zeros((1, length // 2), f32)
            gram_copies = space_copies(gram_buf.at[me], gram_send, gram_recv)
            for copy in gram_copies:
                copy.start()
            for copy in edges_copies:
                copy.wait()

            def image_of(a, carry):
                for c in range(4):
                    padded[c, pl.ds(8, rows), :] = all_ru[a, pl.ds(c * rows, rows), :]
                images[a] = coarse_image(all_edges.at[a])
                return carry

            lax.fori_loop(0, slices, image_of, 0)
    final = bufs[FINE % 2]

    all_rf[tm] = restrict(final, 1, 4)
    sibling = tm + 1 - 2 * lax.rem(tm, 2)

    def rf_copy(slot, index, target):
        return pltpu.make_async_remote_copy(
            src_ref=all_rf.at[slot], dst_ref=all_rf.at[slot],
            send_sem=rf_send.at[index], recv_sem=rf_recv.at[index],
            device_id={"tm": target}, device_id_type=MESH,
        )

    far = [
        rf_copy(tm, off - 1, lax.rem(tm + off, slices)) for off in range(2, slices, 2)
    ]
    near = [rf_copy(tm, 0, sibling)]
    for copy in far + near:
        copy.start()

    def total(buf):
        summed = buf[0]
        for s in range(1, spaces):
            summed = summed + buf[s]
        return jnp.broadcast_to(jnp.sum(summed, axis=1, keepdims=True), summed.shape)

    for copy in gram_copies:
        copy.wait()
    gram = total(gram_buf)
    entry = {}
    line = 0
    for a in range(slices):
        for b in range(a + 1):
            entry[a, b] = gram[line : line + 1]
            line += 1
    factor, inverse = {}, {}
    for b in range(slices):
        diag = entry[b, b]
        for k in range(b):
            diag = diag - factor[b, k] * factor[b, k]
        factor[b, b] = jnp.sqrt(diag)
        inverse[b] = 1.0 / factor[b, b]
        for a in range(b + 1, slices):
            value = entry[a, b]
            for k in range(b):
                value = value - factor[a, k] * factor[b, k]
            factor[a, b] = value * inverse[b]

    for off, copy in zip(range(2, slices, 2), far):
        copy.wait()
        onward = rf_copy(lax.rem(tm - off + slices, slices), off, sibling)
        onward.start()
        near.append(onward)
    for copy in near:
        copy.wait()

    defect_ref[...] = all_rf[0] - all_ru[1]
    for j in range(1, slices):
        turn = j - 1
        layer_out[turn, 0] = defect_ref[pl.ds(per - 1, layers, stride=per), :]
        layer_out[turn, 1] = defect_ref[pl.ds(0, layers, stride=per), :]
        pair = [
            pltpu.make_async_remote_copy(
                src_ref=layer_out.at[turn, way], dst_ref=layer_in.at[turn, way],
                send_sem=layer_send.at[turn, way], recv_sem=layer_recv.at[turn, way],
                device_id={"space": lax.rem(me + by, spaces)}, device_id_type=MESH,
            )
            for way, by in ((0, 1), (1, spaces - 1))
        ]
        start_pair(pair)
        defect = defect_ref[...]
        for a in range(slices):
            dot_buf[turn, me, pl.ds(a, 1), :] = jnp.sum(all_ru[a] * defect, axis=0, keepdims=True)
        for spare in range(slices, dot_buf.shape[2]):
            dot_buf[turn, me, pl.ds(spare, 1), :] = jnp.zeros((1, length // 2), f32)
        copies = space_copies(dot_buf.at[turn, me], dot_send.at[turn], dot_recv.at[turn])
        for copy in copies:
            copy.start()
        if j == 1:
            for a in range(slices):
                images[a] = all_rf[a] - images[a]
        for c in range(4):
            padded[c, pl.ds(8, rows), :] = defect_ref[pl.ds(c * rows, rows), :]
        wait_pair(pair)
        image = coarse_image(layer_in.at[turn])
        if j + 1 < slices:
            defect_ref[...] = all_rf[j] - all_ru[j + 1]
        for copy in copies:
            copy.wait()
        inner = total(dot_buf.at[turn])
        forward, weights = [], [None] * slices
        for a in range(slices):
            value = inner[a : a + 1]
            for k in range(a):
                value = value - factor[a, k] * forward[k]
            forward.append(value * inverse[a])
        for a in reversed(range(slices)):
            value = forward[a]
            for k in range(a + 1, slices):
                value = value - factor[k, a] * weights[k]
            weights[a] = value * inverse[a]
        corr = image
        for a in range(slices):
            corr = corr + weights[a] * images[a]

        @pl.when(tm == j)
        def _():
            corr_ref[...] = corr

        if j + 1 < slices:
            defect_ref[...] = defect_ref[...] + corr

    spread_lo = jnp.where(lane == place // 2, 1.0, 0.0).astype(f32)
    spread_hi = jnp.where(lane == place // 2 + quarter, 1.0, 0.0).astype(f32)
    own = corr_ref[...]
    for buf, spread in ((pair_lo, spread_lo), (pair_hi, spread_hi)):
        wide = jnp.dot(own, spread, precision=lax.Precision.HIGHEST, preferred_element_type=f32)
        buf[pl.ds(0, 4 * rows, stride=2), :] = wide
        buf[pl.ds(1, 4 * rows, stride=2), :] = wide

    def finish(i, carry):
        for c in range(4):
            at = pl.ds(pl.multiple_of((c * half + i) * depth, depth), depth)
            add = jnp.concatenate([pair_lo[at, :], pair_hi[at, :]], axis=1)
            for k in range(2):
                cols = pl.ds(pl.multiple_of((2 * i + k) * length, length), length)
                out_ref[0, c, :, cols] = final[c, 2 * i + k + 1] + add
        return carry

    lax.fori_loop(0, half, finish, 0, unroll=2)


def shards(slices, spaces, starts, labels, coef_table):
    f32 = jnp.float32
    depth, plane = starts.shape[2:]
    length = plane // NX
    width = length // 2
    half = NX // 2
    rows = half * depth // 2
    gram_rows = -(-(slices * (slices + 1) // 2) // 8) * 8
    dot_rows = -(-slices // 8) * 8
    vmem = pl.BlockSpec(memory_space=pltpu.VMEM)
    hbm = pl.BlockSpec(memory_space=pl.ANY)
    dma = pltpu.SemaphoreType.DMA
    return pl.pallas_call(
        functools.partial(kernel, slices, spaces),
        out_shape=jax.ShapeDtypeStruct(starts.shape, f32),
        in_specs=[hbm, hbm, pl.BlockSpec(memory_space=pltpu.SMEM)],
        out_specs=vmem,
        scratch_shapes=[
            pltpu.VMEM(starts.shape, f32),
            pltpu.VMEM(labels.shape, labels.dtype),
            pltpu.VMEM((4, NX + 2, depth, length), f32),
            pltpu.VMEM((4, NX + 2, depth, length), f32),
            pltpu.VMEM((3, NX, depth, length), f32),
            pltpu.VMEM((FINE, 2, 4, NX, 1, length), f32),
            pltpu.VMEM((8 * rows, width), f32),
            pltpu.VMEM((8 * rows, width), f32),
            pltpu.VMEM((3 * rows, width), f32),
            pltpu.VMEM((slices, 4 * rows, width), f32),
            pltpu.VMEM((slices, 4 * rows, width), f32),
            pltpu.VMEM((spaces, gram_rows, width), f32),
            pltpu.VMEM((slices - 1, spaces, dot_rows, width), f32),
            pltpu.VMEM((4, rows + 16, width), f32),
            pltpu.VMEM((2, 4 * rows, width), f32),
            pltpu.VMEM((slices - 1, 2, 4 * half, width), f32),
            pltpu.VMEM((slices - 1, 2, 4 * half, width), f32),
            pltpu.VMEM((4 * rows, width), f32),
            pltpu.VMEM((4 * rows, width), f32),
            dma((FINE, 2, CHUNKS)),
            dma((FINE, 2, CHUNKS)),
            dma((slices - 1,)),
            dma((slices - 1,)),
            dma((slices - 1,)),
            dma((slices - 1,)),
            dma((spaces - 1,)),
            dma((spaces - 1,)),
            dma((slices - 1, spaces - 1)),
            dma((slices - 1, spaces - 1)),
            dma((slices - 1, 2)),
            dma((slices - 1, 2)),
            pltpu.VMEM((2, 4 * half, width), f32),
            pltpu.VMEM((slices, 2, 4 * half, width), f32),
            pltpu.VMEM((slices, 4 * rows, width), f32),
            dma((2,)),
            dma((2,)),
            dma((2,)),
            dma((slices - 1,)),
            dma((slices - 1,)),
        ],
        compiler_params=pltpu.CompilerParams(
            collective_id=0, has_side_effects=True, vmem_limit_bytes=60 * 1024 * 1024
        ),
    )(starts, labels, coef_table)


def solution(mesh):
    placed = (P("tm", None, "space", None), P("space", None), P())
    return jax.shard_map(
        functools.partial(shards, mesh.shape["tm"], mesh.shape["space"]),
        mesh=mesh, in_specs=placed, out_specs=P("tm", None, "space", None), check_vma=False,
    )
```

```python
import functools
import jax
import jax.numpy as jnp
from jax import lax
from jax.experimental import pallas as pl
from jax.experimental.pallas import tpu as pltpu
from jax.sharding import PartitionSpec as P

NX = 32
FINE = 4
CHUNKS = 4
BLOCK = 4

fine_tau = 0.1
coarse_tau = 0.4
MESH = pl.DeviceIdType.MESH


def kernel(
    slices, spaces, starts_hbm, labels_hbm, table_ref, out_ref,
    starts_ref, labels_ref,
    field_a, field_b, coefs, halo, pair_lo, pair_hi, coarse_coefs,
    all_ru, all_rf, gram_buf, dot_buf, padded, expanded, layer_out, layer_in, defect_ref, corr_ref,
    halo_send, halo_recv, ru_send, ru_recv, rf_send, rf_recv,
    gram_send, gram_recv, dot_send, dot_recv, layer_send, layer_recv,
    edges_out, all_edges, images, fetch_sem, edge_send, edge_recv, edges_send, edges_recv,
):
    tm = lax.axis_index("tm")
    me = lax.axis_index("space")
    length = starts_ref.shape[-1] // NX
    depth = starts_ref.shape[2]
    half = NX // 2
    rows = half * depth // 2
    f32 = jnp.float32

    fetch = (
        pltpu.make_async_copy(starts_hbm, starts_ref, fetch_sem.at[0]),
        pltpu.make_async_copy(labels_hbm, labels_ref, fetch_sem.at[1]),
    )
    for copy in fetch:
        copy.start()
    barrier = pltpu.get_barrier_semaphore()
    for off in range(1, slices):
        pl.semaphore_signal(
            barrier, inc=1, device_id={"tm": lax.rem(tm + off, slices)}, device_id_type=MESH
        )
    for off in range(1, spaces):
        pl.semaphore_signal(
            barrier, inc=1, device_id={"space": lax.rem(me + off, spaces)}, device_id_type=MESH
        )

    has_down = me > 0
    has_up = me < spaces - 1

    zero_plane = jnp.zeros((4, 1, depth, length), f32)
    for buf in (field_a, field_b):
        buf[:, pl.ds(0, 1)] = zero_plane
        buf[:, pl.ds(NX + 1, 1)] = zero_plane

    fetch[0].wait()

    def load(x, carry):
        cols = pl.ds(pl.multiple_of(x * length, length), length)
        field_a[:, x + 1] = starts_ref[0, :, :, cols]
        return carry

    lax.fori_loop(0, NX, load, 0, unroll=4)

    span = NX // CHUNKS

    def halo_copies(step, chunk, buf):
        xs = pl.ds(1 + chunk * span, span)
        to = pl.ds(chunk * span, span)
        up = pltpu.make_async_remote_copy(
            src_ref=buf.at[:, xs, pl.ds(depth - 1, 1), :],
            dst_ref=halo.at[step, 0, :, to],
            send_sem=halo_send.at[step, 0, chunk],
            recv_sem=halo_recv.at[step, 0, chunk],
            device_id={"space": lax.rem(me + 1, spaces)},
            device_id_type=MESH,
        )
        down = pltpu.make_async_remote_copy(
            src_ref=buf.at[:, xs, pl.ds(0, 1), :],
            dst_ref=halo.at[step, 1, :, to],
            send_sem=halo_send.at[step, 1, chunk],
            recv_sem=halo_recv.at[step, 1, chunk],
            device_id={"space": lax.rem(me + spaces - 1, spaces)},
            device_id_type=MESH,
        )
        return up, down

    def start_pair(pair):
        @pl.when(has_up)
        def _():
            pair[0].start()

        @pl.when(has_down)
        def _():
            pair[1].start()

    def wait_pair(pair):
        @pl.when(has_up)
        def _():
            pair[0].wait_send()
            pair[1].wait_recv()

        @pl.when(has_down)
        def _():
            pair[1].wait_send()
            pair[0].wait_recv()

    @pl.when(jnp.logical_not(has_down))
    def _():
        for step in range(FINE):
            halo[step, 0] = jnp.zeros(halo.shape[2:], f32)
        for turn in range(slices - 1):
            layer_in[turn, 0] = jnp.zeros(layer_in.shape[2:], f32)
        all_edges[tm, 0] = jnp.zeros(all_edges.shape[2:], f32)

    @pl.when(jnp.logical_not(has_up))
    def _():
        for step in range(FINE):
            halo[step, 1] = jnp.zeros(halo.shape[2:], f32)
        for turn in range(slices - 1):
            layer_in[turn, 1] = jnp.zeros(layer_in.shape[2:], f32)
        all_edges[tm, 1] = jnp.zeros(all_edges.shape[2:], f32)

    fetch[1].wait()
    scales = (fine_tau, fine_tau, fine_tau * 0.5)

    def fill(x, carry):
        cols = pl.ds(pl.multiple_of(x * length, length), length)
        labels = labels_ref[:, cols]
        for k in range(3):
            value = jnp.zeros(labels.shape, f32)
            for tissue in range(table_ref.shape[1]):
                value = jnp.where(labels == tissue, table_ref[k, tissue] * scales[k], value)
            coefs[k, x] = value
        return carry

    lax.fori_loop(0, NX, fill, 0, unroll=2)

    lane = lax.broadcasted_iota(jnp.int32, (length // 2, length // 2), 0)
    place = lax.broadcasted_iota(jnp.int32, (length // 2, length // 2), 1)
    quarter = length // 4
    pick_lo = jnp.where(lane // 2 == place, 0.125, 0.0).astype(f32)
    pick_hi = jnp.where(lane // 2 + quarter == place, 0.125, 0.0).astype(f32)

    def restrict(buf, first, count, pairs=half):
        def pair_up(i, carry):
            for c in range(count):
                both = buf[c, first + 2 * i] + buf[c, first + 2 * i + 1]
                at = pl.ds(pl.multiple_of((c * pairs + i) * depth, depth), depth)
                pair_lo[at, :] = both[:, : length // 2]
                pair_hi[at, :] = both[:, length // 2 :]
            return carry

        lax.fori_loop(0, pairs, pair_up, 0, unroll=4)
        kept = count * pairs * depth // 2
        even = pl.ds(0, kept, stride=2)
        odd = pl.ds(1, kept, stride=2)
        low = pair_lo[even, :] + pair_lo[odd, :]
        high = pair_hi[even, :] + pair_hi[odd, :]
        dot = functools.partial(
            jnp.dot, precision=lax.Precision.HIGHEST, preferred_element_type=f32
        )
        return dot(low, pick_lo) + dot(high, pick_hi)

    def gather_copies(buf, sends, recvs):
        return [
            pltpu.make_async_remote_copy(
                src_ref=buf.at[tm], dst_ref=buf.at[tm],
                send_sem=sends.at[off - 1], recv_sem=recvs.at[off - 1],
                device_id={"tm": lax.rem(tm + off, slices)}, device_id_type=MESH,
            )
            for off in range(1, slices)
        ]

    def space_copies(part, sends, recvs):
        return [
            pltpu.make_async_remote_copy(
                src_ref=part, dst_ref=part,
                send_sem=sends.at[off - 1], recv_sem=recvs.at[off - 1],
                device_id={"space": lax.rem(me + off, spaces)}, device_id_type=MESH,
            )
            for off in range(1, spaces)
        ]

    per = depth // 2
    layers = 4 * half
    own_start = restrict(field_a, 1, 4)
    all_ru[tm] = own_start
    defect_ref[...] = own_start
    edges_out[0] = defect_ref[pl.ds(per - 1, layers, stride=per), :]
    edges_out[1] = defect_ref[pl.ds(0, layers, stride=per), :]
    coarse_coefs[...] = restrict(coefs, 0, 3)
    padded[...] = jnp.zeros(padded.shape, f32)
    corr_ref[...] = jnp.zeros(corr_ref.shape, f32)

    pl.semaphore_wait(barrier, slices - 1 + spaces - 1)
    for chunk in range(CHUNKS):
        start_pair(halo_copies(0, chunk, field_a))
    edge_pair = [
        pltpu.make_async_remote_copy(
            src_ref=edges_out.at[way], dst_ref=all_edges.at[tm, way],
            send_sem=edge_send.at[way], recv_sem=edge_recv.at[way],
            device_id={"space": lax.rem(me + by, spaces)}, device_id_type=MESH,
        )
        for way, by in ((0, 1), (1, spaces - 1))
    ]
    start_pair(edge_pair)
    ru_copies = gather_copies(all_ru, ru_send, ru_recv)
    for copy in ru_copies:
        copy.start()

    crow = lax.broadcasted_iota(jnp.int32, (rows, length // 2), 0)
    ccol = lax.broadcasted_iota(jnp.int32, (rows, length // 2), 1)
    at_top = lax.rem(crow, per) == per - 1
    at_bottom = lax.rem(crow, per) == 0
    lap_scale = coarse_tau / 4.0 / fine_tau
    div_scale = coarse_tau / 4.0 / (fine_tau * 0.5)

    def coarse_part(k):
        return coarse_coefs[pl.ds(k * rows, rows), :]

    def coarse_image(edges):
        expanded[0, pl.ds(0, layers, stride=per), :] = edges[0]
        expanded[1, pl.ds(per - 1, layers, stride=per), :] = edges[1]
        now, dx, dy, dz, lap = [], [], [], [], []
        width = length // 2
        for c in range(4):
            v = padded[c, pl.ds(8, rows), :]
            x_up = padded[c, pl.ds(8 + per, rows), :]
            x_dn = padded[c, pl.ds(8 - per, rows), :]
            y_up = jnp.where(ccol == width - 1, 0.0, pltpu.roll(v, width - 1, 1))
            y_dn = jnp.where(ccol == 0, 0.0, pltpu.roll(v, 1, 1))
            z_up = jnp.where(at_top, expanded[1, pl.ds(c * rows, rows), :], padded[c, pl.ds(9, rows), :])
            z_dn = jnp.where(at_bottom, expanded[0, pl.ds(c * rows, rows), :], padded[c, pl.ds(7, rows), :])
            now.append(v)
            lap.append((x_up + x_dn + y_up + y_dn + z_up + z_dn - 6.0 * v) * lap_scale)
            if c in (0, 3):
                dx.append(x_up - x_dn)
            if c in (1, 3):
                dy.append(y_up - y_dn)
            if c in (2, 3):
                dz.append(z_up - z_dn)
        couple = coarse_part(2) * div_scale
        grads = (dx[1], dy[1], dz[1])
        parts = [now[c] + (coarse_part(0) * lap[c] - couple * grads[c]) for c in range(3)]
        parts.append(now[3] + (coarse_part(1) * lap[3] - couple * (dx[0] + dy[0] + dz[0])))
        return jnp.concatenate(parts, axis=0)

    edges_copies = gather_copies(all_edges, edges_send, edges_recv)

    row = lax.broadcasted_iota(jnp.int32, (1, depth, length), 1)
    col = lax.broadcasted_iota(jnp.int32, (1, depth, length), 2)
    gram_copies = None
    rf_copies = []
    part_rows = rows // CHUNKS

    def end_state(a):
        return all_rf[a].reshape(4 * rows, length // 2)

    bufs = (field_a, field_b)
    for step in range(FINE):
        src, dst = bufs[step % 2], bufs[(step + 1) % 2]
        for chunk in range(CHUNKS):
            wait_pair(halo_copies(step, chunk, src))

            def block(b, carry):
                x0 = chunk * span + b * BLOCK
                now, dx, dy, dz, lap = [], [], [], [], []
                for c in range(4):
                    v = src[c, pl.ds(x0 + 1, BLOCK)]
                    x_up = src[c, pl.ds(x0 + 2, BLOCK)]
                    x_dn = src[c, pl.ds(x0, BLOCK)]
                    y_up = jnp.where(col == length - 1, 0.0, pltpu.roll(v, length - 1, 2))
                    y_dn = jnp.where(col == 0, 0.0, pltpu.roll(v, 1, 2))
                    z_up = jnp.where(
                        row == depth - 1, halo[step, 1, c, pl.ds(x0, BLOCK)], pltpu.roll(v, depth - 1, 1)
                    )
                    z_dn = jnp.where(row == 0, halo[step, 0, c, pl.ds(x0, BLOCK)], pltpu.roll(v, 1, 1))
                    now.append(v)
                    lap.append(x_up + x_dn + y_up + y_dn + z_up + z_dn - 6.0 * v)
                    if c in (0, 3):
                        dx.append(x_up - x_dn)
                    if c in (1, 3):
                        dy.append(y_up - y_dn)
                    if c in (2, 3):
                        dz.append(z_up - z_dn)
                shear = coefs[0, pl.ds(x0, BLOCK)]
                perm = coefs[1, pl.ds(x0, BLOCK)]
                couple = coefs[2, pl.ds(x0, BLOCK)]
                grads = (dx[1], dy[1], dz[1])
                for c in range(3):
                    dst[c, pl.ds(x0 + 1, BLOCK)] = now[c] + (shear * lap[c] - couple * grads[c])
                dst[3, pl.ds(x0 + 1, BLOCK)] = now[3] + (
                    perm * lap[3] - couple * (dx[0] + dy[0] + dz[0])
                )
                return carry

            lax.fori_loop(0, span // BLOCK, block, 0)
            if step + 1 < FINE:
                start_pair(halo_copies(step + 1, chunk, dst))
            else:
                piece = pl.ds(chunk * part_rows, part_rows)
                ends = restrict(dst, 1 + chunk * span, 4, span // 2)
                all_rf[tm, :, piece, :] = ends.reshape(4, part_rows, length // 2)
                sent = [
                    pltpu.make_async_remote_copy(
                        src_ref=all_rf.at[tm, :, piece, :], dst_ref=all_rf.at[tm, :, piece, :],
                        send_sem=rf_send.at[off - 1, chunk], recv_sem=rf_recv.at[off - 1, chunk],
                        device_id={"tm": lax.rem(tm + off, slices)}, device_id_type=MESH,
                    )
                    for off in range(1, slices)
                ]
                for copy in sent:
                    copy.start()
                rf_copies.extend(sent)
        if step == 0:
            wait_pair(edge_pair)
            for copy in edges_copies:
                copy.start()
        if step == FINE - 2:
            for copy in ru_copies:
                copy.wait()
            line = 0
            for a in range(slices):
                for b in range(a + 1):
                    gram_buf[me, pl.ds(line, 1), :] = jnp.sum(
                        all_ru[a] * all_ru[b], axis=0, keepdims=True
                    )
                    line += 1
            for spare in range(line, gram_buf.shape[1]):
                gram_buf[me, pl.ds(spare, 1), :] = jnp.zeros((1, length // 2), f32)
            gram_copies = space_copies(gram_buf.at[me], gram_send, gram_recv)
            for copy in gram_copies:
                copy.start()
            for copy in edges_copies:
                copy.wait()

            def image_of(a, carry):
                for c in range(4):
                    padded[c, pl.ds(8, rows), :] = all_ru[a, pl.ds(c * rows, rows), :]
                images[a] = coarse_image(all_edges.at[a])
                return carry

            lax.fori_loop(0, slices, image_of, 0)
    final = bufs[FINE % 2]

    def total(buf):
        summed = buf[0]
        for s in range(1, spaces):
            summed = summed + buf[s]
        return jnp.broadcast_to(jnp.sum(summed, axis=1, keepdims=True), summed.shape)

    for copy in gram_copies:
        copy.wait()
    gram = total(gram_buf)
    entry = {}
    line = 0
    for a in range(slices):
        for b in range(a + 1):
            entry[a, b] = gram[line : line + 1]
            line += 1
    factor, inverse = {}, {}
    for b in range(slices):
        diag = entry[b, b]
        for k in range(b):
            diag = diag - factor[b, k] * factor[b, k]
        factor[b, b] = jnp.sqrt(diag)
        inverse[b] = 1.0 / factor[b, b]
        for a in range(b + 1, slices):
            value = entry[a, b]
            for k in range(b):
                value = value - factor[a, k] * factor[b, k]
            factor[a, b] = value * inverse[b]

    for copy in rf_copies:
        copy.wait()
    defect_ref[...] = end_state(0) - all_ru[1]
    for j in range(1, slices):
        turn = j - 1
        layer_out[turn, 0] = defect_ref[pl.ds(per - 1, layers, stride=per), :]
        layer_out[turn, 1] = defect_ref[pl.ds(0, layers, stride=per), :]
        pair = [
            pltpu.make_async_remote_copy(
                src_ref=layer_out.at[turn, way], dst_ref=layer_in.at[turn, way],
                send_sem=layer_send.at[turn, way], recv_sem=layer_recv.at[turn, way],
                device_id={"space": lax.rem(me + by, spaces)}, device_id_type=MESH,
            )
            for way, by in ((0, 1), (1, spaces - 1))
        ]
        start_pair(pair)
        defect = defect_ref[...]
        for a in range(slices):
            dot_buf[turn, me, pl.ds(a, 1), :] = jnp.sum(all_ru[a] * defect, axis=0, keepdims=True)
        for spare in range(slices, dot_buf.shape[2]):
            dot_buf[turn, me, pl.ds(spare, 1), :] = jnp.zeros((1, length // 2), f32)
        copies = space_copies(dot_buf.at[turn, me], dot_send.at[turn], dot_recv.at[turn])
        for copy in copies:
            copy.start()
        if j == 1:
            for a in range(slices):
                images[a] = end_state(a) - images[a]
        for c in range(4):
            padded[c, pl.ds(8, rows), :] = defect_ref[pl.ds(c * rows, rows), :]
        wait_pair(pair)
        image = coarse_image(layer_in.at[turn])
        if j + 1 < slices:
            defect_ref[...] = end_state(j) - all_ru[j + 1]
        for copy in copies:
            copy.wait()
        inner = total(dot_buf.at[turn])
        forward, weights = [], [None] * slices
        for a in range(slices):
            value = inner[a : a + 1]
            for k in range(a):
                value = value - factor[a, k] * forward[k]
            forward.append(value * inverse[a])
        for a in reversed(range(slices)):
            value = forward[a]
            for k in range(a + 1, slices):
                value = value - factor[k, a] * weights[k]
            weights[a] = value * inverse[a]
        corr = image
        for a in range(slices):
            corr = corr + weights[a] * images[a]

        @pl.when(tm == j)
        def _():
            corr_ref[...] = corr

        if j + 1 < slices:
            defect_ref[...] = defect_ref[...] + corr

    spread_lo = jnp.where(lane == place // 2, 1.0, 0.0).astype(f32)
    spread_hi = jnp.where(lane == place // 2 + quarter, 1.0, 0.0).astype(f32)
    own = corr_ref[...]
    for buf, spread in ((pair_lo, spread_lo), (pair_hi, spread_hi)):
        wide = jnp.dot(own, spread, precision=lax.Precision.HIGHEST, preferred_element_type=f32)
        buf[pl.ds(0, 4 * rows, stride=2), :] = wide
        buf[pl.ds(1, 4 * rows, stride=2), :] = wide

    def finish(i, carry):
        for c in range(4):
            at = pl.ds(pl.multiple_of((c * half + i) * depth, depth), depth)
            add = jnp.concatenate([pair_lo[at, :], pair_hi[at, :]], axis=1)
            for k in range(2):
                cols = pl.ds(pl.multiple_of((2 * i + k) * length, length), length)
                out_ref[0, c, :, cols] = final[c, 2 * i + k + 1] + add
        return carry

    lax.fori_loop(0, half, finish, 0, unroll=2)


def shards(slices, spaces, starts, labels, coef_table):
    f32 = jnp.float32
    depth, plane = starts.shape[2:]
    length = plane // NX
    width = length // 2
    half = NX // 2
    rows = half * depth // 2
    gram_rows = -(-(slices * (slices + 1) // 2) // 8) * 8
    dot_rows = -(-slices // 8) * 8
    vmem = pl.BlockSpec(memory_space=pltpu.VMEM)
    hbm = pl.BlockSpec(memory_space=pl.ANY)
    dma = pltpu.SemaphoreType.DMA
    return pl.pallas_call(
        functools.partial(kernel, slices, spaces),
        out_shape=jax.ShapeDtypeStruct(starts.shape, f32),
        in_specs=[hbm, hbm, pl.BlockSpec(memory_space=pltpu.SMEM)],
        out_specs=vmem,
        scratch_shapes=[
            pltpu.VMEM(starts.shape, f32),
            pltpu.VMEM(labels.shape, labels.dtype),
            pltpu.VMEM((4, NX + 2, depth, length), f32),
            pltpu.VMEM((4, NX + 2, depth, length), f32),
            pltpu.VMEM((3, NX, depth, length), f32),
            pltpu.VMEM((FINE, 2, 4, NX, 1, length), f32),
            pltpu.VMEM((8 * rows, width), f32),
            pltpu.VMEM((8 * rows, width), f32),
            pltpu.VMEM((3 * rows, width), f32),
            pltpu.VMEM((slices, 4 * rows, width), f32),
            pltpu.VMEM((slices, 4, rows, width), f32),
            pltpu.VMEM((spaces, gram_rows, width), f32),
            pltpu.VMEM((slices - 1, spaces, dot_rows, width), f32),
            pltpu.VMEM((4, rows + 16, width), f32),
            pltpu.VMEM((2, 4 * rows, width), f32),
            pltpu.VMEM((slices - 1, 2, 4 * half, width), f32),
            pltpu.VMEM((slices - 1, 2, 4 * half, width), f32),
            pltpu.VMEM((4 * rows, width), f32),
            pltpu.VMEM((4 * rows, width), f32),
            dma((FINE, 2, CHUNKS)),
            dma((FINE, 2, CHUNKS)),
            dma((slices - 1,)),
            dma((slices - 1,)),
            dma((slices - 1, CHUNKS)),
            dma((slices - 1, CHUNKS)),
            dma((spaces - 1,)),
            dma((spaces - 1,)),
            dma((slices - 1, spaces - 1)),
            dma((slices - 1, spaces - 1)),
            dma((slices - 1, 2)),
            dma((slices - 1, 2)),
            pltpu.VMEM((2, 4 * half, width), f32),
            pltpu.VMEM((slices, 2, 4 * half, width), f32),
            pltpu.VMEM((slices, 4 * rows, width), f32),
            dma((2,)),
            dma((2,)),
            dma((2,)),
            dma((slices - 1,)),
            dma((slices - 1,)),
        ],
        compiler_params=pltpu.CompilerParams(
            collective_id=0, has_side_effects=True, vmem_limit_bytes=60 * 1024 * 1024
        ),
    )(starts, labels, coef_table)


def solution(mesh):
    placed = (P("tm", None, "space", None), P("space", None), P())
    return jax.shard_map(
        functools.partial(shards, mesh.shape["tm"], mesh.shape["space"]),
        mesh=mesh, in_specs=placed, out_specs=P("tm", None, "space", None), check_vma=False,
    )
```

```python
import functools
import jax
import jax.numpy as jnp
from jax import lax
from jax.experimental import pallas as pl
from jax.experimental.pallas import tpu as pltpu
from jax.sharding import PartitionSpec as P

NX = 32
FINE = 4
CHUNKS = 4
BLOCK = 4

fine_tau = 0.1
coarse_tau = 0.4
MESH = pl.DeviceIdType.MESH


def kernel(
    slices, spaces, starts_hbm, labels_hbm, table_ref, out_ref,
    starts_ref, labels_ref,
    field_a, field_b, coefs, halo, pair_lo, pair_hi, coarse_coefs,
    all_ru, all_rf, gram_buf, dot_buf, padded, expanded, layer_out, layer_in, defect_ref, corr_ref,
    halo_send, halo_recv, ru_send, ru_recv, rf_send, rf_recv,
    gram_send, gram_recv, dot_send, dot_recv, layer_send, layer_recv,
    edges_out, all_edges, images, fetch_sem, edge_send, edge_recv, edges_send, edges_recv,
):
    tm = lax.axis_index("tm")
    me = lax.axis_index("space")
    length = starts_ref.shape[-1] // NX
    depth = starts_ref.shape[2]
    half = NX // 2
    rows = half * depth // 2
    f32 = jnp.float32

    fetch = (
        pltpu.make_async_copy(starts_hbm, starts_ref, fetch_sem.at[0]),
        pltpu.make_async_copy(labels_hbm, labels_ref, fetch_sem.at[1]),
    )
    for copy in fetch:
        copy.start()
    barrier = pltpu.get_barrier_semaphore()
    for off in range(1, slices):
        pl.semaphore_signal(
            barrier, inc=1, device_id={"tm": lax.rem(tm + off, slices)}, device_id_type=MESH
        )
    for off in range(1, spaces):
        pl.semaphore_signal(
            barrier, inc=1, device_id={"space": lax.rem(me + off, spaces)}, device_id_type=MESH
        )

    has_down = me > 0
    has_up = me < spaces - 1

    zero_plane = jnp.zeros((4, 1, depth, length), f32)
    for buf in (field_a, field_b):
        buf[:, pl.ds(0, 1)] = zero_plane
        buf[:, pl.ds(NX + 1, 1)] = zero_plane

    fetch[0].wait()

    def load(x, carry):
        cols = pl.ds(pl.multiple_of(x * length, length), length)
        field_a[:, x + 1] = starts_ref[0, :, :, cols]
        return carry

    lax.fori_loop(0, NX, load, 0, unroll=4)

    span = NX // CHUNKS

    def halo_copies(step, chunk, buf):
        xs = pl.ds(1 + chunk * span, span)
        to = pl.ds(chunk * span, span)
        up = pltpu.make_async_remote_copy(
            src_ref=buf.at[:, xs, pl.ds(depth - 1, 1), :],
            dst_ref=halo.at[step, 0, :, to],
            send_sem=halo_send.at[step, 0, chunk],
            recv_sem=halo_recv.at[step, 0, chunk],
            device_id={"space": lax.rem(me + 1, spaces)},
            device_id_type=MESH,
        )
        down = pltpu.make_async_remote_copy(
            src_ref=buf.at[:, xs, pl.ds(0, 1), :],
            dst_ref=halo.at[step, 1, :, to],
            send_sem=halo_send.at[step, 1, chunk],
            recv_sem=halo_recv.at[step, 1, chunk],
            device_id={"space": lax.rem(me + spaces - 1, spaces)},
            device_id_type=MESH,
        )
        return up, down

    def start_pair(pair):
        @pl.when(has_up)
        def _():
            pair[0].start()

        @pl.when(has_down)
        def _():
            pair[1].start()

    def wait_pair(pair):
        @pl.when(has_up)
        def _():
            pair[0].wait_send()
            pair[1].wait_recv()

        @pl.when(has_down)
        def _():
            pair[1].wait_send()
            pair[0].wait_recv()

    @pl.when(jnp.logical_not(has_down))
    def _():
        for step in range(FINE):
            halo[step, 0] = jnp.zeros(halo.shape[2:], f32)
        for turn in range(slices - 1):
            layer_in[turn, 0] = jnp.zeros(layer_in.shape[2:], f32)
        all_edges[tm, 0] = jnp.zeros(all_edges.shape[2:], f32)

    @pl.when(jnp.logical_not(has_up))
    def _():
        for step in range(FINE):
            halo[step, 1] = jnp.zeros(halo.shape[2:], f32)
        for turn in range(slices - 1):
            layer_in[turn, 1] = jnp.zeros(layer_in.shape[2:], f32)
        all_edges[tm, 1] = jnp.zeros(all_edges.shape[2:], f32)

    fetch[1].wait()
    scales = (fine_tau, fine_tau, fine_tau * 0.5)

    def fill(x, carry):
        cols = pl.ds(pl.multiple_of(x * length, length), length)
        labels = labels_ref[:, cols]
        for k in range(3):
            value = jnp.zeros(labels.shape, f32)
            for tissue in range(table_ref.shape[1]):
                value = jnp.where(labels == tissue, table_ref[k, tissue] * scales[k], value)
            coefs[k, x] = value
        return carry

    lax.fori_loop(0, NX, fill, 0, unroll=2)

    lane = lax.broadcasted_iota(jnp.int32, (length // 2, length // 2), 0)
    place = lax.broadcasted_iota(jnp.int32, (length // 2, length // 2), 1)
    quarter = length // 4
    pick_lo = jnp.where(lane // 2 == place, 0.125, 0.0).astype(f32)
    pick_hi = jnp.where(lane // 2 + quarter == place, 0.125, 0.0).astype(f32)

    def restrict(buf, first, count, pairs=half):
        def pair_up(i, carry):
            for c in range(count):
                both = buf[c, first + 2 * i] + buf[c, first + 2 * i + 1]
                at = pl.ds(pl.multiple_of((c * pairs + i) * depth, depth), depth)
                pair_lo[at, :] = both[:, : length // 2]
                pair_hi[at, :] = both[:, length // 2 :]
            return carry

        lax.fori_loop(0, pairs, pair_up, 0, unroll=4)
        kept = count * pairs * depth // 2
        even = pl.ds(0, kept, stride=2)
        odd = pl.ds(1, kept, stride=2)
        low = pair_lo[even, :] + pair_lo[odd, :]
        high = pair_hi[even, :] + pair_hi[odd, :]
        dot = functools.partial(
            jnp.dot, precision=lax.Precision.HIGHEST, preferred_element_type=f32
        )
        return dot(low, pick_lo) + dot(high, pick_hi)

    def gather_copies(buf, sends, recvs):
        return [
            pltpu.make_async_remote_copy(
                src_ref=buf.at[tm], dst_ref=buf.at[tm],
                send_sem=sends.at[off - 1], recv_sem=recvs.at[off - 1],
                device_id={"tm": lax.rem(tm + off, slices)}, device_id_type=MESH,
            )
            for off in range(1, slices)
        ]

    def space_copies(part, sends, recvs):
        return [
            pltpu.make_async_remote_copy(
                src_ref=part, dst_ref=part,
                send_sem=sends.at[off - 1], recv_sem=recvs.at[off - 1],
                device_id={"space": lax.rem(me + off, spaces)}, device_id_type=MESH,
            )
            for off in range(1, spaces)
        ]

    per = depth // 2
    layers = 4 * half
    own_start = restrict(field_a, 1, 4)
    all_ru[tm] = own_start
    defect_ref[...] = own_start
    edges_out[0] = defect_ref[pl.ds(per - 1, layers, stride=per), :]
    edges_out[1] = defect_ref[pl.ds(0, layers, stride=per), :]
    coarse_coefs[...] = restrict(coefs, 0, 3)
    padded[...] = jnp.zeros(padded.shape, f32)
    corr_ref[...] = jnp.zeros(corr_ref.shape, f32)

    pl.semaphore_wait(barrier, slices - 1 + spaces - 1)
    for chunk in range(CHUNKS):
        start_pair(halo_copies(0, chunk, field_a))
    edge_pair = [
        pltpu.make_async_remote_copy(
            src_ref=edges_out.at[way], dst_ref=all_edges.at[tm, way],
            send_sem=edge_send.at[way], recv_sem=edge_recv.at[way],
            device_id={"space": lax.rem(me + by, spaces)}, device_id_type=MESH,
        )
        for way, by in ((0, 1), (1, spaces - 1))
    ]
    start_pair(edge_pair)
    ru_copies = gather_copies(all_ru, ru_send, ru_recv)
    for copy in ru_copies:
        copy.start()

    crow = lax.broadcasted_iota(jnp.int32, (rows, length // 2), 0)
    ccol = lax.broadcasted_iota(jnp.int32, (rows, length // 2), 1)
    at_top = lax.rem(crow, per) == per - 1
    at_bottom = lax.rem(crow, per) == 0
    lap_scale = coarse_tau / 4.0 / fine_tau
    div_scale = coarse_tau / 4.0 / (fine_tau * 0.5)

    def coarse_part(k):
        return coarse_coefs[pl.ds(k * rows, rows), :]

    def coarse_image(edges):
        expanded[0, pl.ds(0, layers, stride=per), :] = edges[0]
        expanded[1, pl.ds(per - 1, layers, stride=per), :] = edges[1]
        now, dx, dy, dz, lap = [], [], [], [], []
        width = length // 2
        for c in range(4):
            v = padded[c, pl.ds(8, rows), :]
            x_up = padded[c, pl.ds(8 + per, rows), :]
            x_dn = padded[c, pl.ds(8 - per, rows), :]
            y_up = jnp.where(ccol == width - 1, 0.0, pltpu.roll(v, width - 1, 1))
            y_dn = jnp.where(ccol == 0, 0.0, pltpu.roll(v, 1, 1))
            z_up = jnp.where(at_top, expanded[1, pl.ds(c * rows, rows), :], padded[c, pl.ds(9, rows), :])
            z_dn = jnp.where(at_bottom, expanded[0, pl.ds(c * rows, rows), :], padded[c, pl.ds(7, rows), :])
            now.append(v)
            lap.append((x_up + x_dn + y_up + y_dn + z_up + z_dn - 6.0 * v) * lap_scale)
            if c in (0, 3):
                dx.append(x_up - x_dn)
            if c in (1, 3):
                dy.append(y_up - y_dn)
            if c in (2, 3):
                dz.append(z_up - z_dn)
        couple = coarse_part(2) * div_scale
        grads = (dx[1], dy[1], dz[1])
        parts = [now[c] + (coarse_part(0) * lap[c] - couple * grads[c]) for c in range(3)]
        parts.append(now[3] + (coarse_part(1) * lap[3] - couple * (dx[0] + dy[0] + dz[0])))
        return jnp.concatenate(parts, axis=0)

    edges_copies = gather_copies(all_edges, edges_send, edges_recv)

    row = lax.broadcasted_iota(jnp.int32, (1, depth, length), 1)
    col = lax.broadcasted_iota(jnp.int32, (1, depth, length), 2)
    gram_copies = None
    rf_copies = []
    part_rows = rows // CHUNKS

    def end_state(a):
        return all_rf[a].reshape(4 * rows, length // 2)

    bufs = (field_a, field_b)
    for step in range(FINE):
        src, dst = bufs[step % 2], bufs[(step + 1) % 2]
        for chunk in range(CHUNKS):
            wait_pair(halo_copies(step, chunk, src))

            def block(b, carry):
                x0 = chunk * span + b * BLOCK
                now, dx, dy, dz, lap = [], [], [], [], []
                for c in range(4):
                    v = src[c, pl.ds(x0 + 1, BLOCK)]
                    x_up = src[c, pl.ds(x0 + 2, BLOCK)]
                    x_dn = src[c, pl.ds(x0, BLOCK)]
                    y_up = jnp.where(col == length - 1, 0.0, pltpu.roll(v, length - 1, 2))
                    y_dn = jnp.where(col == 0, 0.0, pltpu.roll(v, 1, 2))
                    z_up = jnp.where(
                        row == depth - 1, halo[step, 1, c, pl.ds(x0, BLOCK)], pltpu.roll(v, depth - 1, 1)
                    )
                    z_dn = jnp.where(row == 0, halo[step, 0, c, pl.ds(x0, BLOCK)], pltpu.roll(v, 1, 1))
                    now.append(v)
                    lap.append(x_up + x_dn + y_up + y_dn + z_up + z_dn - 6.0 * v)
                    if c in (0, 3):
                        dx.append(x_up - x_dn)
                    if c in (1, 3):
                        dy.append(y_up - y_dn)
                    if c in (2, 3):
                        dz.append(z_up - z_dn)
                shear = coefs[0, pl.ds(x0, BLOCK)]
                perm = coefs[1, pl.ds(x0, BLOCK)]
                couple = coefs[2, pl.ds(x0, BLOCK)]
                grads = (dx[1], dy[1], dz[1])
                for c in range(3):
                    dst[c, pl.ds(x0 + 1, BLOCK)] = now[c] + (shear * lap[c] - couple * grads[c])
                dst[3, pl.ds(x0 + 1, BLOCK)] = now[3] + (
                    perm * lap[3] - couple * (dx[0] + dy[0] + dz[0])
                )
                return carry

            lax.fori_loop(0, span // BLOCK, block, 0)
            if step + 1 < FINE:
                start_pair(halo_copies(step + 1, chunk, dst))
            else:
                piece = pl.ds(chunk * part_rows, part_rows)
                ends = restrict(dst, 1 + chunk * span, 4, span // 2)
                all_rf[tm, :, piece, :] = ends.reshape(4, part_rows, length // 2)
                sent = [
                    pltpu.make_async_remote_copy(
                        src_ref=all_rf.at[tm, :, piece, :], dst_ref=all_rf.at[tm, :, piece, :],
                        send_sem=rf_send.at[off - 1, chunk], recv_sem=rf_recv.at[off - 1, chunk],
                        device_id={"tm": lax.rem(tm + off, slices)}, device_id_type=MESH,
                    )
                    for off in range(1, slices)
                ]
                for copy in sent:
                    copy.start()
                rf_copies.extend(sent)
        if step == 0:
            wait_pair(edge_pair)
            for copy in edges_copies:
                copy.start()
        if step == FINE - 2:
            for copy in ru_copies:
                copy.wait()
            line = 0
            for a in range(slices):
                for b in range(a + 1):
                    gram_buf[me, pl.ds(line, 1), :] = jnp.sum(
                        all_ru[a] * all_ru[b], axis=0, keepdims=True
                    )
                    line += 1
            for spare in range(line, gram_buf.shape[1]):
                gram_buf[me, pl.ds(spare, 1), :] = jnp.zeros((1, length // 2), f32)
            gram_copies = space_copies(gram_buf.at[me], gram_send, gram_recv)
            for copy in gram_copies:
                copy.start()
            for copy in edges_copies:
                copy.wait()

            def image_of(a, carry):
                for c in range(4):
                    padded[c, pl.ds(8, rows), :] = all_ru[a, pl.ds(c * rows, rows), :]
                images[a] = coarse_image(all_edges.at[a])
                return carry

            lax.fori_loop(0, slices, image_of, 0)
    final = bufs[FINE % 2]

    def total(buf):
        summed = buf[0]
        for s in range(1, spaces):
            summed = summed + buf[s]
        return jnp.broadcast_to(jnp.sum(summed, axis=1, keepdims=True), summed.shape)

    for copy in gram_copies:
        copy.wait()
    gram = total(gram_buf)
    entry = {}
    line = 0
    for a in range(slices):
        for b in range(a + 1):
            entry[a, b] = gram[line : line + 1]
            line += 1
    factor, inverse = {}, {}
    for b in range(slices):
        diag = entry[b, b]
        for k in range(b):
            diag = diag - factor[b, k] * factor[b, k]
        factor[b, b] = jnp.sqrt(diag)
        inverse[b] = 1.0 / factor[b, b]
        for a in range(b + 1, slices):
            value = entry[a, b]
            for k in range(b):
                value = value - factor[a, k] * factor[b, k]
            factor[a, b] = value * inverse[b]

    for copy in rf_copies:
        copy.wait()
    defect_ref[...] = end_state(0) - all_ru[1]
    for j in range(1, slices):
        turn = j - 1
        layer_out[turn, 0] = defect_ref[pl.ds(per - 1, layers, stride=per), :]
        layer_out[turn, 1] = defect_ref[pl.ds(0, layers, stride=per), :]
        pair = [
            pltpu.make_async_remote_copy(
                src_ref=layer_out.at[turn, way], dst_ref=layer_in.at[turn, way],
                send_sem=layer_send.at[turn, way], recv_sem=layer_recv.at[turn, way],
                device_id={"space": lax.rem(me + by, spaces)}, device_id_type=MESH,
            )
            for way, by in ((0, 1), (1, spaces - 1))
        ]
        defect = defect_ref[...]
        for a in range(slices):
            dot_buf[turn, me, pl.ds(a, 1), :] = jnp.sum(all_ru[a] * defect, axis=0, keepdims=True)
        for spare in range(slices, dot_buf.shape[2]):
            dot_buf[turn, me, pl.ds(spare, 1), :] = jnp.zeros((1, length // 2), f32)
        copies = space_copies(dot_buf.at[turn, me], dot_send.at[turn], dot_recv.at[turn])
        for copy in copies:
            copy.start()
        start_pair(pair)
        if j == 1:
            for a in range(slices):
                images[a] = end_state(a) - images[a]
        for c in range(4):
            padded[c, pl.ds(8, rows), :] = defect_ref[pl.ds(c * rows, rows), :]
        wait_pair(pair)
        image = coarse_image(layer_in.at[turn])
        if j + 1 < slices:
            defect_ref[...] = end_state(j) - all_ru[j + 1]
        for copy in copies:
            copy.wait()
        inner = total(dot_buf.at[turn])
        forward, weights = [], [None] * slices
        for a in range(slices):
            value = inner[a : a + 1]
            for k in range(a):
                value = value - factor[a, k] * forward[k]
            forward.append(value * inverse[a])
        for a in reversed(range(slices)):
            value = forward[a]
            for k in range(a + 1, slices):
                value = value - factor[k, a] * weights[k]
            weights[a] = value * inverse[a]
        corr = image
        for a in range(slices):
            corr = corr + weights[a] * images[a]

        @pl.when(tm == j)
        def _():
            corr_ref[...] = corr

        if j + 1 < slices:
            defect_ref[...] = defect_ref[...] + corr

    spread_lo = jnp.where(lane == place // 2, 1.0, 0.0).astype(f32)
    spread_hi = jnp.where(lane == place // 2 + quarter, 1.0, 0.0).astype(f32)
    own = corr_ref[...]
    for buf, spread in ((pair_lo, spread_lo), (pair_hi, spread_hi)):
        wide = jnp.dot(own, spread, precision=lax.Precision.HIGHEST, preferred_element_type=f32)
        buf[pl.ds(0, 4 * rows, stride=2), :] = wide
        buf[pl.ds(1, 4 * rows, stride=2), :] = wide

    def finish(i, carry):
        for c in range(4):
            at = pl.ds(pl.multiple_of((c * half + i) * depth, depth), depth)
            add = jnp.concatenate([pair_lo[at, :], pair_hi[at, :]], axis=1)
            for k in range(2):
                cols = pl.ds(pl.multiple_of((2 * i + k) * length, length), length)
                out_ref[0, c, :, cols] = final[c, 2 * i + k + 1] + add
        return carry

    lax.fori_loop(0, half, finish, 0, unroll=2)


def shards(slices, spaces, starts, labels, coef_table):
    f32 = jnp.float32
    depth, plane = starts.shape[2:]
    length = plane // NX
    width = length // 2
    half = NX // 2
    rows = half * depth // 2
    gram_rows = -(-(slices * (slices + 1) // 2) // 8) * 8
    dot_rows = -(-slices // 8) * 8
    vmem = pl.BlockSpec(memory_space=pltpu.VMEM)
    hbm = pl.BlockSpec(memory_space=pl.ANY)
    dma = pltpu.SemaphoreType.DMA
    return pl.pallas_call(
        functools.partial(kernel, slices, spaces),
        out_shape=jax.ShapeDtypeStruct(starts.shape, f32),
        in_specs=[hbm, hbm, pl.BlockSpec(memory_space=pltpu.SMEM)],
        out_specs=vmem,
        scratch_shapes=[
            pltpu.VMEM(starts.shape, f32),
            pltpu.VMEM(labels.shape, labels.dtype),
            pltpu.VMEM((4, NX + 2, depth, length), f32),
            pltpu.VMEM((4, NX + 2, depth, length), f32),
            pltpu.VMEM((3, NX, depth, length), f32),
            pltpu.VMEM((FINE, 2, 4, NX, 1, length), f32),
            pltpu.VMEM((8 * rows, width), f32),
            pltpu.VMEM((8 * rows, width), f32),
            pltpu.VMEM((3 * rows, width), f32),
            pltpu.VMEM((slices, 4 * rows, width), f32),
            pltpu.VMEM((slices, 4, rows, width), f32),
            pltpu.VMEM((spaces, gram_rows, width), f32),
            pltpu.VMEM((slices - 1, spaces, dot_rows, width), f32),
            pltpu.VMEM((4, rows + 16, width), f32),
            pltpu.VMEM((2, 4 * rows, width), f32),
            pltpu.VMEM((slices - 1, 2, 4 * half, width), f32),
            pltpu.VMEM((slices - 1, 2, 4 * half, width), f32),
            pltpu.VMEM((4 * rows, width), f32),
            pltpu.VMEM((4 * rows, width), f32),
            dma((FINE, 2, CHUNKS)),
            dma((FINE, 2, CHUNKS)),
            dma((slices - 1,)),
            dma((slices - 1,)),
            dma((slices - 1, CHUNKS)),
            dma((slices - 1, CHUNKS)),
            dma((spaces - 1,)),
            dma((spaces - 1,)),
            dma((slices - 1, spaces - 1)),
            dma((slices - 1, spaces - 1)),
            dma((slices - 1, 2)),
            dma((slices - 1, 2)),
            pltpu.VMEM((2, 4 * half, width), f32),
            pltpu.VMEM((slices, 2, 4 * half, width), f32),
            pltpu.VMEM((slices, 4 * rows, width), f32),
            dma((2,)),
            dma((2,)),
            dma((2,)),
            dma((slices - 1,)),
            dma((slices - 1,)),
        ],
        compiler_params=pltpu.CompilerParams(
            collective_id=0, has_side_effects=True, vmem_limit_bytes=60 * 1024 * 1024
        ),
    )(starts, labels, coef_table)


def solution(mesh):
    placed = (P("tm", None, "space", None), P("space", None), P())
    return jax.shard_map(
        functools.partial(shards, mesh.shape["tm"], mesh.shape["space"]),
        mesh=mesh, in_specs=placed, out_specs=P("tm", None, "space", None), check_vma=False,
    )
```

```python
import functools
import jax
import jax.numpy as jnp
from jax import lax
from jax.experimental import pallas as pl
from jax.experimental.pallas import tpu as pltpu
from jax.sharding import PartitionSpec as P

NX = 32
FINE = 4
CHUNKS = 4
BLOCK = 4

fine_tau = 0.1
coarse_tau = 0.4
MESH = pl.DeviceIdType.MESH


def kernel(
    slices, spaces, starts_hbm, labels_hbm, table_ref, out_ref,
    starts_ref, labels_ref,
    field_a, field_b, coefs, halo, pair_lo, pair_hi, coarse_coefs,
    all_ru, all_rf, gram_buf, dot_buf, padded, expanded, layer_out, layer_in, defect_ref, corr_ref,
    halo_send, halo_recv, ru_send, ru_recv, rf_send, rf_recv,
    gram_send, gram_recv, dot_send, dot_recv, layer_send, layer_recv,
    edges_out, all_edges, images, fetch_sem, edge_send, edge_recv, edges_send, edges_recv,
):
    tm = lax.axis_index("tm")
    me = lax.axis_index("space")
    length = starts_ref.shape[-1] // NX
    depth = starts_ref.shape[2]
    half = NX // 2
    rows = half * depth // 2
    f32 = jnp.float32

    fetch = (
        pltpu.make_async_copy(starts_hbm, starts_ref, fetch_sem.at[0]),
        pltpu.make_async_copy(labels_hbm, labels_ref, fetch_sem.at[1]),
    )
    for copy in fetch:
        copy.start()
    barrier = pltpu.get_barrier_semaphore()
    for off in range(1, slices):
        pl.semaphore_signal(
            barrier, inc=1, device_id={"tm": lax.rem(tm + off, slices)}, device_id_type=MESH
        )
    for off in range(1, spaces):
        pl.semaphore_signal(
            barrier, inc=1, device_id={"space": lax.rem(me + off, spaces)}, device_id_type=MESH
        )

    has_down = me > 0
    has_up = me < spaces - 1

    zero_plane = jnp.zeros((4, 1, depth, length), f32)
    for buf in (field_a, field_b):
        buf[:, pl.ds(0, 1)] = zero_plane
        buf[:, pl.ds(NX + 1, 1)] = zero_plane

    fetch[0].wait()

    def load(x, carry):
        cols = pl.ds(pl.multiple_of(x * length, length), length)
        field_a[:, x + 1] = starts_ref[0, :, :, cols]
        return carry

    lax.fori_loop(0, NX, load, 0, unroll=4)

    span = NX // CHUNKS

    def halo_copies(step, chunk, buf):
        xs = pl.ds(1 + chunk * span, span)
        to = pl.ds(chunk * span, span)
        up = pltpu.make_async_remote_copy(
            src_ref=buf.at[:, xs, pl.ds(depth - 1, 1), :],
            dst_ref=halo.at[step, 0, :, to],
            send_sem=halo_send.at[step, 0, chunk],
            recv_sem=halo_recv.at[step, 0, chunk],
            device_id={"space": lax.rem(me + 1, spaces)},
            device_id_type=MESH,
        )
        down = pltpu.make_async_remote_copy(
            src_ref=buf.at[:, xs, pl.ds(0, 1), :],
            dst_ref=halo.at[step, 1, :, to],
            send_sem=halo_send.at[step, 1, chunk],
            recv_sem=halo_recv.at[step, 1, chunk],
            device_id={"space": lax.rem(me + spaces - 1, spaces)},
            device_id_type=MESH,
        )
        return up, down

    def start_pair(pair):
        @pl.when(has_up)
        def _():
            pair[0].start()

        @pl.when(has_down)
        def _():
            pair[1].start()

    def wait_pair(pair):
        @pl.when(has_up)
        def _():
            pair[0].wait_send()
            pair[1].wait_recv()

        @pl.when(has_down)
        def _():
            pair[1].wait_send()
            pair[0].wait_recv()

    @pl.when(jnp.logical_not(has_down))
    def _():
        for step in range(FINE):
            halo[step, 0] = jnp.zeros(halo.shape[2:], f32)
        for turn in range(slices - 1):
            layer_in[turn, 0] = jnp.zeros(layer_in.shape[2:], f32)
        all_edges[tm, 0] = jnp.zeros(all_edges.shape[2:], f32)

    @pl.when(jnp.logical_not(has_up))
    def _():
        for step in range(FINE):
            halo[step, 1] = jnp.zeros(halo.shape[2:], f32)
        for turn in range(slices - 1):
            layer_in[turn, 1] = jnp.zeros(layer_in.shape[2:], f32)
        all_edges[tm, 1] = jnp.zeros(all_edges.shape[2:], f32)

    fetch[1].wait()
    scales = (fine_tau, fine_tau, fine_tau * 0.5)

    def fill(x, carry):
        cols = pl.ds(pl.multiple_of(x * length, length), length)
        labels = labels_ref[:, cols]
        for k in range(3):
            value = jnp.zeros(labels.shape, f32)
            for tissue in range(table_ref.shape[1]):
                value = jnp.where(labels == tissue, table_ref[k, tissue] * scales[k], value)
            coefs[k, x] = value
        return carry

    lax.fori_loop(0, NX, fill, 0, unroll=2)

    lane = lax.broadcasted_iota(jnp.int32, (length // 2, length // 2), 0)
    place = lax.broadcasted_iota(jnp.int32, (length // 2, length // 2), 1)
    quarter = length // 4
    pick_lo = jnp.where(lane // 2 == place, 0.125, 0.0).astype(f32)
    pick_hi = jnp.where(lane // 2 + quarter == place, 0.125, 0.0).astype(f32)

    def restrict(buf, first, count, pairs=half):
        def pair_up(i, carry):
            for c in range(count):
                both = buf[c, first + 2 * i] + buf[c, first + 2 * i + 1]
                at = pl.ds(pl.multiple_of((c * pairs + i) * depth, depth), depth)
                pair_lo[at, :] = both[:, : length // 2]
                pair_hi[at, :] = both[:, length // 2 :]
            return carry

        lax.fori_loop(0, pairs, pair_up, 0, unroll=4)
        kept = count * pairs * depth // 2
        even = pl.ds(0, kept, stride=2)
        odd = pl.ds(1, kept, stride=2)
        low = pair_lo[even, :] + pair_lo[odd, :]
        high = pair_hi[even, :] + pair_hi[odd, :]
        dot = functools.partial(
            jnp.dot, precision=lax.Precision.HIGHEST, preferred_element_type=f32
        )
        return dot(low, pick_lo) + dot(high, pick_hi)

    def gather_copies(buf, sends, recvs):
        return [
            pltpu.make_async_remote_copy(
                src_ref=buf.at[tm], dst_ref=buf.at[tm],
                send_sem=sends.at[off - 1], recv_sem=recvs.at[off - 1],
                device_id={"tm": lax.rem(tm + off, slices)}, device_id_type=MESH,
            )
            for off in range(1, slices)
        ]

    def space_copies(part, sends, recvs):
        return [
            pltpu.make_async_remote_copy(
                src_ref=part, dst_ref=part,
                send_sem=sends.at[off - 1], recv_sem=recvs.at[off - 1],
                device_id={"space": lax.rem(me + off, spaces)}, device_id_type=MESH,
            )
            for off in sorted(range(1, spaces), key=lambda off: abs(2 * off - spaces))
        ]

    per = depth // 2
    layers = 4 * half
    own_start = restrict(field_a, 1, 4)
    all_ru[tm] = own_start
    defect_ref[...] = own_start
    edges_out[0] = defect_ref[pl.ds(per - 1, layers, stride=per), :]
    edges_out[1] = defect_ref[pl.ds(0, layers, stride=per), :]
    coarse_coefs[...] = restrict(coefs, 0, 3)
    padded[...] = jnp.zeros(padded.shape, f32)
    corr_ref[...] = jnp.zeros(corr_ref.shape, f32)

    pl.semaphore_wait(barrier, slices - 1 + spaces - 1)
    for chunk in range(CHUNKS):
        start_pair(halo_copies(0, chunk, field_a))
    edge_pair = [
        pltpu.make_async_remote_copy(
            src_ref=edges_out.at[way], dst_ref=all_edges.at[tm, way],
            send_sem=edge_send.at[way], recv_sem=edge_recv.at[way],
            device_id={"space": lax.rem(me + by, spaces)}, device_id_type=MESH,
        )
        for way, by in ((0, 1), (1, spaces - 1))
    ]
    start_pair(edge_pair)
    ru_copies = gather_copies(all_ru, ru_send, ru_recv)
    for copy in ru_copies:
        copy.start()

    crow = lax.broadcasted_iota(jnp.int32, (rows, length // 2), 0)
    ccol = lax.broadcasted_iota(jnp.int32, (rows, length // 2), 1)
    at_top = lax.rem(crow, per) == per - 1
    at_bottom = lax.rem(crow, per) == 0
    lap_scale = coarse_tau / 4.0 / fine_tau
    div_scale = coarse_tau / 4.0 / (fine_tau * 0.5)

    def coarse_part(k):
        return coarse_coefs[pl.ds(k * rows, rows), :]

    def coarse_image(edges):
        expanded[0, pl.ds(0, layers, stride=per), :] = edges[0]
        expanded[1, pl.ds(per - 1, layers, stride=per), :] = edges[1]
        now, dx, dy, dz, lap = [], [], [], [], []
        width = length // 2
        for c in range(4):
            v = padded[c, pl.ds(8, rows), :]
            x_up = padded[c, pl.ds(8 + per, rows), :]
            x_dn = padded[c, pl.ds(8 - per, rows), :]
            y_up = jnp.where(ccol == width - 1, 0.0, pltpu.roll(v, width - 1, 1))
            y_dn = jnp.where(ccol == 0, 0.0, pltpu.roll(v, 1, 1))
            z_up = jnp.where(at_top, expanded[1, pl.ds(c * rows, rows), :], padded[c, pl.ds(9, rows), :])
            z_dn = jnp.where(at_bottom, expanded[0, pl.ds(c * rows, rows), :], padded[c, pl.ds(7, rows), :])
            now.append(v)
            lap.append((x_up + x_dn + y_up + y_dn + z_up + z_dn - 6.0 * v) * lap_scale)
            if c in (0, 3):
                dx.append(x_up - x_dn)
            if c in (1, 3):
                dy.append(y_up - y_dn)
            if c in (2, 3):
                dz.append(z_up - z_dn)
        couple = coarse_part(2) * div_scale
        grads = (dx[1], dy[1], dz[1])
        parts = [now[c] + (coarse_part(0) * lap[c] - couple * grads[c]) for c in range(3)]
        parts.append(now[3] + (coarse_part(1) * lap[3] - couple * (dx[0] + dy[0] + dz[0])))
        return jnp.concatenate(parts, axis=0)

    edges_copies = gather_copies(all_edges, edges_send, edges_recv)

    row = lax.broadcasted_iota(jnp.int32, (1, depth, length), 1)
    col = lax.broadcasted_iota(jnp.int32, (1, depth, length), 2)
    gram_copies = None
    rf_copies = []
    part_rows = rows // CHUNKS

    def end_state(a):
        return all_rf[a].reshape(4 * rows, length // 2)

    bufs = (field_a, field_b)
    for step in range(FINE):
        src, dst = bufs[step % 2], bufs[(step + 1) % 2]
        for chunk in range(CHUNKS):
            wait_pair(halo_copies(step, chunk, src))

            def block(b, carry):
                x0 = chunk * span + b * BLOCK
                now, dx, dy, dz, lap = [], [], [], [], []
                for c in range(4):
                    v = src[c, pl.ds(x0 + 1, BLOCK)]
                    x_up = src[c, pl.ds(x0 + 2, BLOCK)]
                    x_dn = src[c, pl.ds(x0, BLOCK)]
                    y_up = jnp.where(col == length - 1, 0.0, pltpu.roll(v, length - 1, 2))
                    y_dn = jnp.where(col == 0, 0.0, pltpu.roll(v, 1, 2))
                    z_up = jnp.where(
                        row == depth - 1, halo[step, 1, c, pl.ds(x0, BLOCK)], pltpu.roll(v, depth - 1, 1)
                    )
                    z_dn = jnp.where(row == 0, halo[step, 0, c, pl.ds(x0, BLOCK)], pltpu.roll(v, 1, 1))
                    now.append(v)
                    lap.append(x_up + x_dn + y_up + y_dn + z_up + z_dn - 6.0 * v)
                    if c in (0, 3):
                        dx.append(x_up - x_dn)
                    if c in (1, 3):
                        dy.append(y_up - y_dn)
                    if c in (2, 3):
                        dz.append(z_up - z_dn)
                shear = coefs[0, pl.ds(x0, BLOCK)]
                perm = coefs[1, pl.ds(x0, BLOCK)]
                couple = coefs[2, pl.ds(x0, BLOCK)]
                grads = (dx[1], dy[1], dz[1])
                for c in range(3):
                    dst[c, pl.ds(x0 + 1, BLOCK)] = now[c] + (shear * lap[c] - couple * grads[c])
                dst[3, pl.ds(x0 + 1, BLOCK)] = now[3] + (
                    perm * lap[3] - couple * (dx[0] + dy[0] + dz[0])
                )
                return carry

            lax.fori_loop(0, span // BLOCK, block, 0)
            if step + 1 < FINE:
                start_pair(halo_copies(step + 1, chunk, dst))
            else:
                piece = pl.ds(chunk * part_rows, part_rows)
                ends = restrict(dst, 1 + chunk * span, 4, span // 2)
                all_rf[tm, :, piece, :] = ends.reshape(4, part_rows, length // 2)
                sent = [
                    pltpu.make_async_remote_copy(
                        src_ref=all_rf.at[tm, :, piece, :], dst_ref=all_rf.at[tm, :, piece, :],
                        send_sem=rf_send.at[off - 1, chunk], recv_sem=rf_recv.at[off - 1, chunk],
                        device_id={"tm": lax.rem(tm + off, slices)}, device_id_type=MESH,
                    )
                    for off in range(1, slices)
                ]
                for copy in sent:
                    copy.start()
                rf_copies.extend(sent)
        if step == 0:
            wait_pair(edge_pair)
            for copy in edges_copies:
                copy.start()
        if step == FINE - 2:
            for copy in ru_copies:
                copy.wait()
            line = 0
            for a in range(slices):
                for b in range(a + 1):
                    gram_buf[me, pl.ds(line, 1), :] = jnp.sum(
                        all_ru[a] * all_ru[b], axis=0, keepdims=True
                    )
                    line += 1
            for spare in range(line, gram_buf.shape[1]):
                gram_buf[me, pl.ds(spare, 1), :] = jnp.zeros((1, length // 2), f32)
            gram_copies = space_copies(gram_buf.at[me], gram_send, gram_recv)
            for copy in gram_copies:
                copy.start()
            for copy in edges_copies:
                copy.wait()

            def image_of(a, carry):
                for c in range(4):
                    padded[c, pl.ds(8, rows), :] = all_ru[a, pl.ds(c * rows, rows), :]
                images[a] = coarse_image(all_edges.at[a])
                return carry

            lax.fori_loop(0, slices, image_of, 0)
    final = bufs[FINE % 2]

    def total(buf):
        summed = buf[0]
        for s in range(1, spaces):
            summed = summed + buf[s]
        return jnp.broadcast_to(jnp.sum(summed, axis=1, keepdims=True), summed.shape)

    for copy in gram_copies:
        copy.wait()
    gram = total(gram_buf)
    entry = {}
    line = 0
    for a in range(slices):
        for b in range(a + 1):
            entry[a, b] = gram[line : line + 1]
            line += 1
    factor, inverse = {}, {}
    for b in range(slices):
        diag = entry[b, b]
        for k in range(b):
            diag = diag - factor[b, k] * factor[b, k]
        factor[b, b] = jnp.sqrt(diag)
        inverse[b] = 1.0 / factor[b, b]
        for a in range(b + 1, slices):
            value = entry[a, b]
            for k in range(b):
                value = value - factor[a, k] * factor[b, k]
            factor[a, b] = value * inverse[b]

    for copy in rf_copies:
        copy.wait()
    defect_ref[...] = end_state(0) - all_ru[1]
    for j in range(1, slices):
        turn = j - 1
        layer_out[turn, 0] = defect_ref[pl.ds(per - 1, layers, stride=per), :]
        layer_out[turn, 1] = defect_ref[pl.ds(0, layers, stride=per), :]
        pair = [
            pltpu.make_async_remote_copy(
                src_ref=layer_out.at[turn, way], dst_ref=layer_in.at[turn, way],
                send_sem=layer_send.at[turn, way], recv_sem=layer_recv.at[turn, way],
                device_id={"space": lax.rem(me + by, spaces)}, device_id_type=MESH,
            )
            for way, by in ((0, 1), (1, spaces - 1))
        ]
        defect = defect_ref[...]
        for a in range(slices):
            dot_buf[turn, me, pl.ds(a, 1), :] = jnp.sum(all_ru[a] * defect, axis=0, keepdims=True)
        for spare in range(slices, dot_buf.shape[2]):
            dot_buf[turn, me, pl.ds(spare, 1), :] = jnp.zeros((1, length // 2), f32)
        copies = space_copies(dot_buf.at[turn, me], dot_send.at[turn], dot_recv.at[turn])
        for copy in copies:
            copy.start()
        start_pair(pair)
        if j == 1:
            for a in range(slices):
                images[a] = end_state(a) - images[a]
        for c in range(4):
            padded[c, pl.ds(8, rows), :] = defect_ref[pl.ds(c * rows, rows), :]
        wait_pair(pair)
        image = coarse_image(layer_in.at[turn])
        if j + 1 < slices:
            defect_ref[...] = end_state(j) - all_ru[j + 1]
        for copy in copies:
            copy.wait()
        inner = total(dot_buf.at[turn])
        forward, weights = [], [None] * slices
        for a in range(slices):
            value = inner[a : a + 1]
            for k in range(a):
                value = value - factor[a, k] * forward[k]
            forward.append(value * inverse[a])
        for a in reversed(range(slices)):
            value = forward[a]
            for k in range(a + 1, slices):
                value = value - factor[k, a] * weights[k]
            weights[a] = value * inverse[a]
        corr = image
        for a in range(slices):
            corr = corr + weights[a] * images[a]

        @pl.when(tm == j)
        def _():
            corr_ref[...] = corr

        if j + 1 < slices:
            defect_ref[...] = defect_ref[...] + corr

    spread_lo = jnp.where(lane == place // 2, 1.0, 0.0).astype(f32)
    spread_hi = jnp.where(lane == place // 2 + quarter, 1.0, 0.0).astype(f32)
    own = corr_ref[...]
    for buf, spread in ((pair_lo, spread_lo), (pair_hi, spread_hi)):
        wide = jnp.dot(own, spread, precision=lax.Precision.HIGHEST, preferred_element_type=f32)
        buf[pl.ds(0, 4 * rows, stride=2), :] = wide
        buf[pl.ds(1, 4 * rows, stride=2), :] = wide

    def finish(i, carry):
        for c in range(4):
            at = pl.ds(pl.multiple_of((c * half + i) * depth, depth), depth)
            add = jnp.concatenate([pair_lo[at, :], pair_hi[at, :]], axis=1)
            for k in range(2):
                cols = pl.ds(pl.multiple_of((2 * i + k) * length, length), length)
                out_ref[0, c, :, cols] = final[c, 2 * i + k + 1] + add
        return carry

    lax.fori_loop(0, half, finish, 0, unroll=2)


def shards(slices, spaces, starts, labels, coef_table):
    f32 = jnp.float32
    depth, plane = starts.shape[2:]
    length = plane // NX
    width = length // 2
    half = NX // 2
    rows = half * depth // 2
    gram_rows = -(-(slices * (slices + 1) // 2) // 8) * 8
    dot_rows = -(-slices // 8) * 8
    vmem = pl.BlockSpec(memory_space=pltpu.VMEM)
    hbm = pl.BlockSpec(memory_space=pl.ANY)
    dma = pltpu.SemaphoreType.DMA
    return pl.pallas_call(
        functools.partial(kernel, slices, spaces),
        out_shape=jax.ShapeDtypeStruct(starts.shape, f32),
        in_specs=[hbm, hbm, pl.BlockSpec(memory_space=pltpu.SMEM)],
        out_specs=vmem,
        scratch_shapes=[
            pltpu.VMEM(starts.shape, f32),
            pltpu.VMEM(labels.shape, labels.dtype),
            pltpu.VMEM((4, NX + 2, depth, length), f32),
            pltpu.VMEM((4, NX + 2, depth, length), f32),
            pltpu.VMEM((3, NX, depth, length), f32),
            pltpu.VMEM((FINE, 2, 4, NX, 1, length), f32),
            pltpu.VMEM((8 * rows, width), f32),
            pltpu.VMEM((8 * rows, width), f32),
            pltpu.VMEM((3 * rows, width), f32),
            pltpu.VMEM((slices, 4 * rows, width), f32),
            pltpu.VMEM((slices, 4, rows, width), f32),
            pltpu.VMEM((spaces, gram_rows, width), f32),
            pltpu.VMEM((slices - 1, spaces, dot_rows, width), f32),
            pltpu.VMEM((4, rows + 16, width), f32),
            pltpu.VMEM((2, 4 * rows, width), f32),
            pltpu.VMEM((slices - 1, 2, 4 * half, width), f32),
            pltpu.VMEM((slices - 1, 2, 4 * half, width), f32),
            pltpu.VMEM((4 * rows, width), f32),
            pltpu.VMEM((4 * rows, width), f32),
            dma((FINE, 2, CHUNKS)),
            dma((FINE, 2, CHUNKS)),
            dma((slices - 1,)),
            dma((slices - 1,)),
            dma((slices - 1, CHUNKS)),
            dma((slices - 1, CHUNKS)),
            dma((spaces - 1,)),
            dma((spaces - 1,)),
            dma((slices - 1, spaces - 1)),
            dma((slices - 1, spaces - 1)),
            dma((slices - 1, 2)),
            dma((slices - 1, 2)),
            pltpu.VMEM((2, 4 * half, width), f32),
            pltpu.VMEM((slices, 2, 4 * half, width), f32),
            pltpu.VMEM((slices, 4 * rows, width), f32),
            dma((2,)),
            dma((2,)),
            dma((2,)),
            dma((slices - 1,)),
            dma((slices - 1,)),
        ],
        compiler_params=pltpu.CompilerParams(
            collective_id=0, has_side_effects=True, vmem_limit_bytes=60 * 1024 * 1024
        ),
    )(starts, labels, coef_table)


def solution(mesh):
    placed = (P("tm", None, "space", None), P("space", None), P())
    return jax.shard_map(
        functools.partial(shards, mesh.shape["tm"], mesh.shape["space"]),
        mesh=mesh, in_specs=placed, out_specs=P("tm", None, "space", None), check_vma=False,
    )
```
